32 devices in a mesh: grp: 2 (over x), cuts: 16 (over z, y, core).
Axes of the slice: x: 2, y: 2, z: 4, core: 2. Of those that a mesh axis runs over, the one named last changes fastest.
Arguments:
- stem_tensor: bfloat16 [2, 128, 32, 512], P(None, ('grp', 'cuts')), parts along dimension 1
- branch_tensors: bfloat16 [2, 2, 2, 512, 512], replicated, may hold values from -0.1875 to 0.1875
- cut_values: int32 [128, 2], P(('grp', 'cuts')), parts along dimension 0, may hold values from 0 to 1
- bit_rows: int32 [16384], P('grp'), parts along dimension 0, may hold values from 0 to 31
- bit_cols: int32 [16384], P('grp'), parts along dimension 0, may hold values from 0 to 511
Outputs:
- amplitudes: float32 [2, 16384], P(None, ('grp', 'cuts')), parts along dimension 1
- log_scale: float32 [2], P('grp'), parts along dimension 0
The draws below stay inside these ranges and needn't reach their ends.
There are 2 independent parts, one for each index of `grp`. The reference program is written for one: setup_inputs(seed, part) draws one part's arguments, and reference() takes and returns one part's arrays. A program takes and returns all parts, laid end to end along the dimension named above; an argument that names none is the same for every part. Nothing has to cross between parts.
All inputs are finite; a program needn't handle non-finite values.
Results may differ from the reference program's by a relative error of at most 0.007.
Values sent between devices are 32-bit elements; how exact they have to be, the bound alone decides.
A program may use at most 128 MiB of HBM per device.

```python
import jax
import jax.numpy as jnp
from jax import lax

K = 512
R = 32
STEPS = 2
SLICES = 64
NB = 8192


def draw_stem_tensor(key, part):
    first, second, third = jax.random.split(key, 3)
    order = jnp.arange(SLICES, dtype=jnp.float32)
    rising = jnp.exp(jnp.log(4.0) * order / max(SLICES - 1, 1))
    rough = jax.random.uniform(second, (SLICES,), jnp.float32, 0.6, 1.6)
    row_scale = jnp.exp(jax.random.uniform(third, (SLICES, R), jnp.float32, 0.0, jnp.log(10.0)))
    base = jax.random.normal(first, (2, SLICES, R, K), jnp.float32)
    values = base * (rising * rough)[None, :, None, None] * row_scale[None, :, :, None] / 4.0
    return values.astype(jnp.bfloat16)


def place_ends(array, rng, least, high):
    shape = array.shape
    spot = [jax.random.randint(jax.random.fold_in(rng, axis), (), 0, shape[axis]) for axis in range(len(shape))]
    array = array.at[tuple(spot)].set(least)
    longest = shape.index(max(shape))
    spot[longest] = (spot[longest] + 1) % shape[longest]
    return array.at[tuple(spot)].set(high)


def normal_values(rng, shape, width, reach, kind=jnp.bfloat16):
    result = jax.random.normal(rng, shape, jnp.float32) * width
    return jnp.minimum(jnp.maximum(result, -reach), reach).astype(kind)


def setup_inputs(seed: int = 0, part: int = 0) -> dict:
    key_list = jax.random.split(jax.random.key(seed), 6)
    part_splits = jax.random.split(jax.random.fold_in(key_list[5], part), 6)
    return {
        "stem_tensor": draw_stem_tensor(jax.random.fold_in(jax.random.fold_in(key_list[5], part), 71), part),
        "branch_tensors": normal_values(key_list[1], (STEPS, 2, 2, K, K), (2 * K) ** -0.5, 0.1875),
        "cut_values": place_ends(jax.random.randint(part_splits[2], (SLICES, STEPS), 0, 2), jax.random.fold_in(part_splits[2], 1), 0, 1).astype(jnp.int32),
        "bit_rows": place_ends(jax.random.randint(part_splits[3], (NB,), 0, R), jax.random.fold_in(part_splits[3], 1), 0, R - 1).astype(jnp.int32),
        "bit_cols": place_ends(jax.random.randint(part_splits[4], (NB,), 0, K), jax.random.fold_in(part_splits[4], 1), 0, K - 1).astype(jnp.int32),
    }


def reference(stem_tensor, branch_tensors, cut_values, bit_rows, bit_cols):
    state = jnp.moveaxis(stem_tensor, 1, 0)
    log_scale = jnp.zeros((1,), jnp.float32)
    table = jnp.zeros((2, R, K), jnp.float32)
    for step in range(STEPS):
        matrices = branch_tensors[step]

        def one_slice(pair):
            piece, value = pair
            chosen = lax.dynamic_index_in_dim(matrices, value, 0, keepdims=False)
            real_part = jnp.dot(piece[0], chosen[0], preferred_element_type=jnp.float32) - jnp.dot(piece[1], chosen[1], preferred_element_type=jnp.float32)
            imag_part = jnp.dot(piece[0], chosen[1], preferred_element_type=jnp.float32) + jnp.dot(piece[1], chosen[0], preferred_element_type=jnp.float32)
            return jnp.stack([real_part, imag_part])
        product = lax.map(one_slice, (state, cut_values[:, step]))
        peak = jnp.sqrt(jnp.max(product[:, 0] * product[:, 0] + product[:, 1] * product[:, 1])) + 1e-06
        log_scale = log_scale + jnp.log(peak)
        if step + 1 < STEPS:
            state = (product / peak).astype(jnp.bfloat16)
        else:
            table = lax.optimization_barrier(jnp.sum(product, axis=0)) / peak
    amplitudes = table[:, bit_rows, bit_cols]
    return (amplitudes, log_scale)
```

```python
import functools

import jax
import jax.numpy as jnp
from jax import lax
from jax.experimental import pallas as pl
from jax.experimental.pallas import tpu as pltpu
from jax.sharding import PartitionSpec as P

LANES = 128
LIFT = 2.0 ** 20


def complex_step(real_part, imag_part, weights):
    upper = jnp.concatenate([real_part, -imag_part], axis=1)
    lower = jnp.concatenate([imag_part, real_part], axis=1)
    left = jnp.concatenate([upper, lower], axis=0)
    return jnp.dot(left, weights, preferred_element_type=jnp.float32)


def largest(values):
    return jnp.max(jnp.max(values, axis=0, keepdims=True), axis=1, keepdims=True)


def kernel(n, group, cut_hbm, stem_hbm, branch_hbm, rows_hbm, cols_hbm, amp_ref, log_ref,
           cut_s, stem_v, early_v, later_v, rows_v, cols_v, outgoing, incoming, load_sems, send_sems, recv_sems):
    me = lax.axis_index("cuts")
    slices, rows, width = stem_hbm.shape[1], stem_hbm.shape[2], stem_hbm.shape[3]
    mine = amp_ref.shape[1]
    lines = mine // LANES

    stem_load = pltpu.make_async_copy(stem_hbm, stem_v, load_sems.at[0])
    cut_load = pltpu.make_async_copy(cut_hbm, cut_s, load_sems.at[1])
    rows_load = pltpu.make_async_copy(rows_hbm, rows_v, load_sems.at[2])
    cols_load = pltpu.make_async_copy(cols_hbm, cols_v, load_sems.at[3])
    branch_loads = [
        pltpu.make_async_copy(branch_hbm.at[step], held, load_sems.at[4 + step])
        for step, held in enumerate((early_v, later_v))
    ]
    cut_load.start()
    stem_load.start()
    branch_loads[0].start()
    cols_load.start()
    rows_load.start()
    branch_loads[1].start()

    barrier = pltpu.get_barrier_semaphore()

    def greet(k, carry):
        pl.semaphore_signal(barrier, inc=1, device_id={"cuts": lax.rem(me + k, n)}, device_id_type=pl.DeviceIdType.MESH)
        return carry

    lax.fori_loop(1, n, greet, 0)

    cut_load.wait()
    stem_load.wait()
    branch_loads[0].wait()
    first = []
    for s in range(slices):
        weights = early_v[cut_s[0, s]].reshape(2 * width, width)
        first.append(complex_step(stem_v[0, s], stem_v[1, s], weights))
    branch_loads[1].wait()
    second = []
    for s in range(slices):
        state = (first[s] * LIFT).astype(jnp.bfloat16)
        weights = later_v[cut_s[1, s]].reshape(2 * width, width)
        second.append(complex_step(state[:rows], state[rows:], weights))

    square = functools.reduce(jnp.maximum, [p[:rows] * p[:rows] + p[rows:] * p[rows:] for p in first])
    peak_square = largest(square)
    own_peak = jnp.sqrt(peak_square) + 1e-06
    shrink = (1.0 / LIFT) / own_peak
    shrunk = [p * shrink for p in second]
    square = functools.reduce(jnp.maximum, [p[:rows] * p[:rows] + p[rows:] * p[rows:] for p in shrunk])
    raw_second = jnp.sqrt(largest(square)) * own_peak
    stats = jnp.concatenate(
        [jnp.broadcast_to(peak_square, (1, LANES)), jnp.broadcast_to(raw_second, (1, LANES))], axis=0)

    table = functools.reduce(jnp.add, second)
    high = table.astype(jnp.bfloat16)
    low = (table - high.astype(jnp.float32)).astype(jnp.bfloat16)
    left = jnp.concatenate([high, low], axis=0)

    cols_load.wait()
    rows_load.wait()
    pl.semaphore_wait(barrier, n - 1)

    def picked(dest):
        col_lines = cols_v[dest]
        row_lines = rows_v[dest]
        column = lax.broadcasted_iota(jnp.int32, (width, LANES), 0)
        row = lax.broadcasted_iota(jnp.int32, (rows, LANES), 0)
        hot = jnp.concatenate(
            [jnp.where(column == col_lines[j:j + 1], 1.0, 0.0).astype(jnp.bfloat16) for j in range(lines)], axis=1)
        found = jnp.dot(left, hot, preferred_element_type=jnp.float32)
        found = found[:2 * rows] + found[2 * rows:]
        chosen = jnp.concatenate([row == row_lines[j:j + 1] for j in range(lines)], axis=1)
        parts = [jnp.sum(jnp.where(chosen, found[p * rows:(p + 1) * rows], 0.0), axis=0, keepdims=True) for p in range(2)]
        return jnp.concatenate(parts, axis=0)

    def remote(dest):
        return pltpu.make_async_remote_copy(
            src_ref=outgoing.at[dest],
            dst_ref=incoming.at[me],
            send_sem=send_sems.at[dest],
            recv_sem=recv_sems.at[me],
            device_id={"cuts": dest},
            device_id_type=pl.DeviceIdType.MESH,
        )

    def serve(start, count):
        dests = [lax.rem(me + start + i, n) for i in range(count)]
        for dest in dests:
            outgoing[dest, :, :mine] = picked(dest)
            outgoing[dest, :, mine:] = stats
        for dest in dests:
            remote(dest).start()

    def serve_group(g, carry):
        serve(1 + g * group, group)
        return carry

    rounds = (n - 1) // group
    lax.fori_loop(0, rounds, serve_group, 0)
    serve(1 + rounds * group, n - 1 - rounds * group)
    incoming[me, :, :mine] = picked(me)
    incoming[me, :, mine:] = stats

    def receive(k, carry):
        source = lax.rem(me + k, n)
        pltpu.make_async_remote_copy(
            src_ref=outgoing.at[source],
            dst_ref=incoming.at[source],
            send_sem=send_sems.at[source],
            recv_sem=recv_sems.at[source],
            device_id={"cuts": source},
            device_id_type=pl.DeviceIdType.MESH,
        ).wait()
        return carry

    lax.fori_loop(1, n, receive, 0)
    total = jnp.sum(incoming[:, :, :mine], axis=0)
    peaks = jnp.max(incoming[:, :, mine:], axis=0)
    first_peak = jnp.sqrt(peaks[0:1, 0:1]) + 1e-06
    second_peak = peaks[1:2, 0:1] / first_peak + 1e-06
    amp_ref[...] = total * ((1.0 / LIFT) / first_peak) / second_peak
    log_ref[...] = jnp.log(first_peak) + jnp.log(second_peak)


def shards(stem_tensor, branch_tensors, cut_values, bit_rows, bit_cols):
    n = lax.axis_size("cuts")
    slices = stem_tensor.shape[1]
    mine = bit_rows.shape[0] // n
    steps = branch_tensors.shape[0]
    any_spec = pl.BlockSpec(memory_space=pl.ANY)
    lined = (n, mine // LANES, LANES)
    amplitudes, log_scale = pl.pallas_call(
        functools.partial(kernel, n, 5),
        out_shape=(
            jax.ShapeDtypeStruct((2, mine), jnp.float32),
            jax.ShapeDtypeStruct((1, 1), jnp.float32),
        ),
        in_specs=[any_spec] * 5,
        out_specs=(pl.BlockSpec(memory_space=pltpu.VMEM), pl.BlockSpec(memory_space=pltpu.VMEM)),
        scratch_shapes=[
            pltpu.SMEM((steps, slices), jnp.int32),
            pltpu.VMEM(stem_tensor.shape, jnp.bfloat16),
            pltpu.VMEM(branch_tensors.shape[1:], jnp.bfloat16),
            pltpu.VMEM(branch_tensors.shape[1:], jnp.bfloat16),
            pltpu.VMEM(lined, jnp.int32),
            pltpu.VMEM(lined, jnp.int32),
            pltpu.VMEM((n, 2, mine + LANES), jnp.float32),
            pltpu.VMEM((n, 2, mine + LANES), jnp.float32),
            pltpu.SemaphoreType.DMA((4 + steps,)),
            pltpu.SemaphoreType.DMA((n,)),
            pltpu.SemaphoreType.DMA((n,)),
        ],
        compiler_params=pltpu.CompilerParams(
            collective_id=0, has_side_effects=True, vmem_limit_bytes=56 * 1024 * 1024
        ),
    )(cut_values.T, stem_tensor, branch_tensors, bit_rows.reshape(lined), bit_cols.reshape(lined))
    return (amplitudes, log_scale.reshape(1))


def solution(mesh):
    placed = (
        P(None, ("grp", "cuts"), None, None),
        P(),
        P(("grp", "cuts"), None),
        P("grp"),
        P("grp"),
    )
    return jax.shard_map(
        shards,
        mesh=mesh,
        in_specs=placed,
        out_specs=(P(None, ("grp", "cuts")), P("grp")),
        check_vma=False,
    )
```

```python
import functools

import jax
import jax.numpy as jnp
from jax import lax
from jax.experimental import pallas as pl
from jax.experimental.pallas import tpu as pltpu
from jax.sharding import PartitionSpec as P

LANES = 128
LIFT = 2.0 ** 20


def complex_step(real_part, imag_part, weights):
    upper = jnp.concatenate([real_part, -imag_part], axis=1)
    lower = jnp.concatenate([imag_part, real_part], axis=1)
    left = jnp.concatenate([upper, lower], axis=0)
    return jnp.dot(left, weights, preferred_element_type=jnp.float32)


def largest(values):
    return jnp.max(jnp.max(values, axis=0, keepdims=True), axis=1, keepdims=True)


def kernel(n, group, cut_hbm, stem_hbm, branch_hbm, rows_hbm, cols_hbm, out_ref,
           cut_s, stem_v, early_v, later_v, rows_v, cols_v, outgoing, incoming, load_sems, send_sems, recv_sems):
    me = lax.axis_index("cuts")
    slices, rows, width = stem_hbm.shape[1], stem_hbm.shape[2], stem_hbm.shape[3]
    mine = out_ref.shape[1] - LANES
    lines = mine // LANES

    stem_load = pltpu.make_async_copy(stem_hbm, stem_v, load_sems.at[0])
    cut_load = pltpu.make_async_copy(cut_hbm, cut_s, load_sems.at[1])
    rows_load = pltpu.make_async_copy(rows_hbm, rows_v, load_sems.at[2])
    cols_load = pltpu.make_async_copy(cols_hbm, cols_v, load_sems.at[3])
    branch_loads = [
        pltpu.make_async_copy(branch_hbm.at[step], held, load_sems.at[4 + step])
        for step, held in enumerate((early_v, later_v))
    ]
    cut_load.start()
    stem_load.start()
    branch_loads[0].start()
    cols_load.start()
    rows_load.start()
    branch_loads[1].start()

    barrier = pltpu.get_barrier_semaphore()

    def greet(k, carry):
        pl.semaphore_signal(barrier, inc=1, device_id={"cuts": lax.rem(me + k, n)}, device_id_type=pl.DeviceIdType.MESH)
        return carry

    lax.fori_loop(1, n, greet, 0)

    cut_load.wait()
    stem_load.wait()
    branch_loads[0].wait()
    first = []
    for s in range(slices):
        weights = early_v[cut_s[0, s]].reshape(2 * width, width)
        first.append(complex_step(stem_v[0, s], stem_v[1, s], weights))
    branch_loads[1].wait()
    second = []
    for s in range(slices):
        state = (first[s] * LIFT).astype(jnp.bfloat16)
        weights = later_v[cut_s[1, s]].reshape(2 * width, width)
        second.append(complex_step(state[:rows], state[rows:], weights))

    square = functools.reduce(jnp.maximum, [p[:rows] * p[:rows] + p[rows:] * p[rows:] for p in first])
    peak_square = largest(square)
    own_peak = jnp.sqrt(peak_square) + 1e-06
    shrink = (1.0 / LIFT) / own_peak
    shrunk = [p * shrink for p in second]
    square = functools.reduce(jnp.maximum, [p[:rows] * p[:rows] + p[rows:] * p[rows:] for p in shrunk])
    raw_second = jnp.sqrt(largest(square)) * own_peak
    stats = jnp.concatenate(
        [jnp.broadcast_to(peak_square, (1, LANES)), jnp.broadcast_to(raw_second, (1, LANES))], axis=0)

    table = functools.reduce(jnp.add, second)
    high = table.astype(jnp.bfloat16)
    low = (table - high.astype(jnp.float32)).astype(jnp.bfloat16)
    left = jnp.concatenate([high, low], axis=0)

    cols_load.wait()
    rows_load.wait()
    pl.semaphore_wait(barrier, n - 1)

    def picked(dest):
        col_lines = cols_v[dest]
        row_lines = rows_v[dest]
        column = lax.broadcasted_iota(jnp.int32, (width, LANES), 0)
        row = lax.broadcasted_iota(jnp.int32, (rows, LANES), 0)
        hot = jnp.concatenate(
            [jnp.where(column == col_lines[j:j + 1], 1.0, 0.0).astype(jnp.bfloat16) for j in range(lines)], axis=1)
        found = jnp.dot(left, hot, preferred_element_type=jnp.float32)
        found = found[:2 * rows] + found[2 * rows:]
        chosen = jnp.concatenate([row == row_lines[j:j + 1] for j in range(lines)], axis=1)
        parts = [jnp.sum(jnp.where(chosen, found[p * rows:(p + 1) * rows], 0.0), axis=0, keepdims=True) for p in range(2)]
        return jnp.concatenate(parts, axis=0)

    def remote(dest):
        return pltpu.make_async_remote_copy(
            src_ref=outgoing.at[dest],
            dst_ref=incoming.at[me],
            send_sem=send_sems.at[dest],
            recv_sem=recv_sems.at[me],
            device_id={"cuts": dest},
            device_id_type=pl.DeviceIdType.MESH,
        )

    def serve(start, count):
        dests = [lax.rem(me + start + i, n) for i in range(count)]
        for dest in dests:
            outgoing[dest, :, :mine] = picked(dest)
            outgoing[dest, :, mine:] = stats
        for dest in dests:
            remote(dest).start()

    def serve_group(g, carry):
        serve(1 + g * group, group)
        return carry

    rounds = (n - 1) // group
    lax.fori_loop(0, rounds, serve_group, 0)
    serve(1 + rounds * group, n - 1 - rounds * group)
    incoming[me, :, :mine] = picked(me)
    incoming[me, :, mine:] = stats

    def receive(k, carry):
        source = lax.rem(me + k, n)
        pltpu.make_async_remote_copy(
            src_ref=outgoing.at[source],
            dst_ref=incoming.at[source],
            send_sem=send_sems.at[source],
            recv_sem=recv_sems.at[source],
            device_id={"cuts": source},
            device_id_type=pl.DeviceIdType.MESH,
        ).wait()
        return carry

    lax.fori_loop(1, n, receive, 0)
    out_ref[:, :mine] = jnp.sum(incoming[:, :, :mine], axis=0)
    out_ref[:, mine:] = jnp.max(incoming[:, :, mine:], axis=0)


def finish(sum_ref, amp_hbm, log_hbm, amp_v, log_v, sems):
    mine = amp_v.shape[1]
    peaks = sum_ref[:, mine:]
    first_peak = jnp.sqrt(peaks[0:1, 0:1]) + 1e-06
    second_peak = peaks[1:2, 0:1] / first_peak + 1e-06
    log_v[...] = jnp.log(first_peak) + jnp.log(second_peak)
    log_store = pltpu.make_async_copy(log_v, log_hbm, sems.at[0])
    log_store.start()
    amp_v[...] = sum_ref[:, :mine] * ((1.0 / LIFT) / first_peak) / second_peak
    amp_store = pltpu.make_async_copy(amp_v, amp_hbm, sems.at[1])
    amp_store.start()
    log_store.wait()
    amp_store.wait()


def shards(stem_tensor, branch_tensors, cut_values, bit_rows, bit_cols):
    n = lax.axis_size("cuts")
    slices = stem_tensor.shape[1]
    mine = bit_rows.shape[0] // n
    steps = branch_tensors.shape[0]
    any_spec = pl.BlockSpec(memory_space=pl.ANY)
    lined = (n, mine // LANES, LANES)
    sums = pl.pallas_call(
        functools.partial(kernel, n, 5),
        out_shape=pltpu.VMEM((2, mine + LANES), jnp.float32),
        in_specs=[any_spec] * 5,
        out_specs=pl.BlockSpec(memory_space=pltpu.VMEM),
        scratch_shapes=[
            pltpu.SMEM((steps, slices), jnp.int32),
            pltpu.VMEM(stem_tensor.shape, jnp.bfloat16),
            pltpu.VMEM(branch_tensors.shape[1:], jnp.bfloat16),
            pltpu.VMEM(branch_tensors.shape[1:], jnp.bfloat16),
            pltpu.VMEM(lined, jnp.int32),
            pltpu.VMEM(lined, jnp.int32),
            pltpu.VMEM((n, 2, mine + LANES), jnp.float32),
            pltpu.VMEM((n, 2, mine + LANES), jnp.float32),
            pltpu.SemaphoreType.DMA((4 + steps,)),
            pltpu.SemaphoreType.DMA((n,)),
            pltpu.SemaphoreType.DMA((n,)),
        ],
        compiler_params=pltpu.CompilerParams(
            collective_id=0, has_side_effects=True, vmem_limit_bytes=56 * 1024 * 1024
        ),
    )(cut_values.T, stem_tensor, branch_tensors, bit_rows.reshape(lined), bit_cols.reshape(lined))
    amplitudes, log_scale = pl.pallas_call(
        finish,
        out_shape=(
            jax.ShapeDtypeStruct((2, mine), jnp.float32),
            jax.ShapeDtypeStruct((1, 1), jnp.float32),
        ),
        in_specs=[pl.BlockSpec(memory_space=pltpu.VMEM)],
        out_specs=(any_spec, any_spec),
        scratch_shapes=[
            pltpu.VMEM((2, mine), jnp.float32),
            pltpu.VMEM((1, 1), jnp.float32),
            pltpu.SemaphoreType.DMA((2,)),
        ],
    )(sums)
    return (amplitudes, log_scale.reshape(1))


def solution(mesh):
    placed = (
        P(None, ("grp", "cuts"), None, None),
        P(),
        P(("grp", "cuts"), None),
        P("grp"),
        P("grp"),
    )
    return jax.shard_map(
        shards,
        mesh=mesh,
        in_specs=placed,
        out_specs=(P(None, ("grp", "cuts")), P("grp")),
        check_vma=False,
    )
```

```python
import functools

import jax
import jax.numpy as jnp
from jax import lax
from jax.experimental import pallas as pl
from jax.experimental.pallas import tpu as pltpu
from jax.sharding import PartitionSpec as P

LANES = 128
LIFT = 2.0 ** 20


def complex_step(real_part, imag_part, weights):
    upper = jnp.concatenate([real_part, -imag_part], axis=1)
    lower = jnp.concatenate([imag_part, real_part], axis=1)
    left = jnp.concatenate([upper, lower], axis=0)
    return jnp.dot(left, weights, preferred_element_type=jnp.float32)


def largest(values):
    return jnp.max(jnp.max(values, axis=0, keepdims=True), axis=1, keepdims=True)


def kernel(n, group, cut_hbm, stem_hbm, branch_hbm, rows_hbm, cols_hbm, out_ref,
           cut_s, stem_v, early_v, later_v, rows_v, cols_v, hot_v, outgoing, incoming, load_sems, send_sems, recv_sems):
    me = lax.axis_index("cuts")
    slices, rows, width = stem_hbm.shape[1], stem_hbm.shape[2], stem_hbm.shape[3]
    mine = out_ref.shape[1] - LANES
    lines = mine // LANES

    cols_load = pltpu.make_async_copy(cols_hbm, cols_v, load_sems.at[0])
    rows_load = pltpu.make_async_copy(rows_hbm, rows_v, load_sems.at[1])
    cut_load = pltpu.make_async_copy(cut_hbm, cut_s, load_sems.at[2])
    stem_load = pltpu.make_async_copy(stem_hbm, stem_v, load_sems.at[3])
    branch_loads = [
        [
            pltpu.make_async_copy(
                branch_hbm.at[step, value, part], held.at[value, part], load_sems.at[4 + 4 * step + 2 * value + part])
            for value in range(2) for part in range(2)
        ]
        for step, held in enumerate((early_v, later_v))
    ]
    for load in [cols_load, stem_load, cut_load] + branch_loads[0] + [rows_load] + branch_loads[1]:
        load.start()

    barrier = pltpu.get_barrier_semaphore()

    def greet(k, carry):
        pl.semaphore_signal(barrier, inc=1, device_id={"cuts": lax.rem(me + k, n)}, device_id_type=pl.DeviceIdType.MESH)
        return carry

    lax.fori_loop(1, n, greet, 0)

    def hot_columns(dest):
        col_lines = cols_v[dest]
        column = lax.broadcasted_iota(jnp.int16, (width, LANES), 0)
        one, zero = jnp.bfloat16(1), jnp.bfloat16(0)
        lanes = [jnp.broadcast_to(col_lines[j:j + 1], (width, LANES)).astype(jnp.int16) for j in range(lines)]
        return jnp.concatenate([jnp.where(column == line, one, zero) for line in lanes], axis=1)

    def keep_hot(k, carry):
        hot_v[k] = hot_columns(lax.rem(me + 1 + k, n))
        return carry

    cols_load.wait()
    if hot_v.shape[0] == n:
        lax.fori_loop(0, n, keep_hot, 0)

    cut_load.wait()
    stem_load.wait()
    for load in branch_loads[0]:
        load.wait()
    first = []
    for s in range(slices):
        weights = early_v[cut_s[0, s]].reshape(2 * width, width)
        first.append(complex_step(stem_v[0, s], stem_v[1, s], weights))
    for load in branch_loads[1]:
        load.wait()
    second = []
    for s in range(slices):
        state = (first[s] * LIFT).astype(jnp.bfloat16)
        weights = later_v[cut_s[1, s]].reshape(2 * width, width)
        second.append(complex_step(state[:rows], state[rows:], weights))

    square = functools.reduce(jnp.maximum, [p[:rows] * p[:rows] + p[rows:] * p[rows:] for p in first])
    peak_square = largest(square)
    own_peak = jnp.sqrt(peak_square) + 1e-06
    shrink = (1.0 / LIFT) / own_peak
    shrunk = [p * shrink for p in second]
    square = functools.reduce(jnp.maximum, [p[:rows] * p[:rows] + p[rows:] * p[rows:] for p in shrunk])
    raw_second = jnp.sqrt(largest(square)) * own_peak
    stats = jnp.concatenate(
        [jnp.broadcast_to(peak_square, (1, LANES)), jnp.broadcast_to(raw_second, (1, LANES))], axis=0)

    table = functools.reduce(jnp.add, second)
    high = table.astype(jnp.bfloat16)
    low = (table - high.astype(jnp.float32)).astype(jnp.bfloat16)
    left = jnp.concatenate([high, low], axis=0)

    rows_load.wait()
    pl.semaphore_wait(barrier, n - 1)

    def picked(dest, hot):
        row_lines = rows_v[dest]
        row = lax.broadcasted_iota(jnp.int32, (rows, LANES), 0)
        found = jnp.dot(left, hot, preferred_element_type=jnp.float32)
        found = found[:2 * rows] + found[2 * rows:]
        chosen = jnp.concatenate([row == row_lines[j:j + 1] for j in range(lines)], axis=1)
        parts = [jnp.sum(jnp.where(chosen, found[p * rows:(p + 1) * rows], 0.0), axis=0, keepdims=True) for p in range(2)]
        return jnp.concatenate(parts, axis=0)

    def remote(dest):
        return pltpu.make_async_remote_copy(
            src_ref=outgoing.at[dest],
            dst_ref=incoming.at[me],
            send_sem=send_sems.at[dest],
            recv_sem=recv_sems.at[me],
            device_id={"cuts": dest},
            device_id_type=pl.DeviceIdType.MESH,
        )

    def serve(start, count):
        dests = [lax.rem(me + 1 + start + i, n) for i in range(count)]
        for i, dest in enumerate(dests):
            hot = hot_v[start + i] if hot_v.shape[0] == n else hot_columns(dest)
            outgoing[dest, :, :mine] = picked(dest, hot)
            outgoing[dest, :, mine:] = stats
        for dest in dests:
            remote(dest).start()

    def serve_group(g, carry):
        serve(g * group, group)
        return carry

    rounds = (n - 1) // group
    if hot_v.shape[0] == n:
        for g in range(rounds):
            serve(g * group, group)
    else:
        lax.fori_loop(0, rounds, serve_group, 0)
    serve(rounds * group, n - 1 - rounds * group)
    incoming[me, :, :mine] = picked(me, hot_v[n - 1] if hot_v.shape[0] == n else hot_columns(me))
    incoming[me, :, mine:] = stats

    def receive(k, carry):
        source = lax.rem(me + k, n)
        pltpu.make_async_remote_copy(
            src_ref=outgoing.at[source],
            dst_ref=incoming.at[source],
            send_sem=send_sems.at[source],
            recv_sem=recv_sems.at[source],
            device_id={"cuts": source},
            device_id_type=pl.DeviceIdType.MESH,
        ).wait()
        return carry

    lax.fori_loop(1, n, receive, 0)
    out_ref[:, :mine] = jnp.sum(incoming[:, :, :mine], axis=0)
    out_ref[:, mine:] = jnp.max(incoming[:, :, mine:], axis=0)


def finish(sum_ref, amp_hbm, log_hbm, amp_v, log_v, sems):
    mine = amp_v.shape[1]
    peaks = sum_ref[:, mine:]
    first_peak = jnp.sqrt(peaks[0:1, 0:1]) + 1e-06
    second_peak = peaks[1:2, 0:1] / first_peak + 1e-06
    log_v[...] = jnp.log(first_peak) + jnp.log(second_peak)
    log_store = pltpu.make_async_copy(log_v, log_hbm, sems.at[0])
    log_store.start()
    amp_v[...] = sum_ref[:, :mine] * ((1.0 / LIFT) / first_peak) / second_peak
    amp_store = pltpu.make_async_copy(amp_v, amp_hbm, sems.at[1])
    amp_store.start()
    log_store.wait()
    amp_store.wait()


def shards(stem_tensor, branch_tensors, cut_values, bit_rows, bit_cols):
    n = lax.axis_size("cuts")
    slices = stem_tensor.shape[1]
    mine = bit_rows.shape[0] // n
    steps = branch_tensors.shape[0]
    width = stem_tensor.shape[3]
    any_spec = pl.BlockSpec(memory_space=pl.ANY)
    lined = (n, mine // LANES, LANES)
    sums = pl.pallas_call(
        functools.partial(kernel, n, 3),
        out_shape=pltpu.VMEM((2, mine + LANES), jnp.float32),
        in_specs=[any_spec] * 5,
        out_specs=pl.BlockSpec(memory_space=pltpu.VMEM),
        scratch_shapes=[
            pltpu.SMEM((steps, slices), jnp.int32),
            pltpu.VMEM(stem_tensor.shape, jnp.bfloat16),
            pltpu.VMEM(branch_tensors.shape[1:], jnp.bfloat16),
            pltpu.VMEM(branch_tensors.shape[1:], jnp.bfloat16),
            pltpu.VMEM(lined, jnp.int32),
            pltpu.VMEM(lined, jnp.int32),
            pltpu.VMEM((n if n <= 16 else 1, width, mine), jnp.bfloat16),
            pltpu.VMEM((n, 2, mine + LANES), jnp.float32),
            pltpu.VMEM((n, 2, mine + LANES), jnp.float32),
            pltpu.SemaphoreType.DMA((4 + 4 * steps,)),
            pltpu.SemaphoreType.DMA((n,)),
            pltpu.SemaphoreType.DMA((n,)),
        ],
        compiler_params=pltpu.CompilerParams(
            collective_id=0, has_side_effects=True, vmem_limit_bytes=56 * 1024 * 1024
        ),
    )(cut_values.T, stem_tensor, branch_tensors, bit_rows.reshape(lined), bit_cols.reshape(lined))
    amplitudes, log_scale = pl.pallas_call(
        finish,
        out_shape=(
            jax.ShapeDtypeStruct((2, mine), jnp.float32),
            jax.ShapeDtypeStruct((1, 1), jnp.float32),
        ),
        in_specs=[pl.BlockSpec(memory_space=pltpu.VMEM)],
        out_specs=(any_spec, any_spec),
        scratch_shapes=[
            pltpu.VMEM((2, mine), jnp.float32),
            pltpu.VMEM((1, 1), jnp.float32),
            pltpu.SemaphoreType.DMA((2,)),
        ],
    )(pltpu.with_memory_space_constraint(sums, pltpu.VMEM))
    return (amplitudes, log_scale.reshape(1))


def solution(mesh):
    placed = (
        P(None, ("grp", "cuts"), None, None),
        P(),
        P(("grp", "cuts"), None),
        P("grp"),
        P("grp"),
    )
    return jax.shard_map(
        shards,
        mesh=mesh,
        in_specs=placed,
        out_specs=(P(None, ("grp", "cuts")), P("grp")),
        check_vma=False,
    )
```

```python
import functools

import jax
import jax.numpy as jnp
from jax import lax
from jax.experimental import pallas as pl
from jax.experimental.pallas import tpu as pltpu
from jax.sharding import PartitionSpec as P

LANES = 128
LIFT = 2.0 ** 20


def complex_step(real_part, imag_part, weights):
    upper = jnp.concatenate([real_part, -imag_part], axis=1)
    lower = jnp.concatenate([imag_part, real_part], axis=1)
    left = jnp.concatenate([upper, lower], axis=0)
    return jnp.dot(left, weights, preferred_element_type=jnp.float32)


def largest(values):
    return jnp.max(jnp.max(values, axis=0, keepdims=True), axis=1, keepdims=True)


def kernel(n, group, cut_hbm, stem_hbm, branch_hbm, rows_hbm, cols_hbm, out_ref,
           cut_s, stem_v, early_v, later_v, rows_v, cols_v, hot_v, outgoing, incoming, load_sems, send_sem, recv_sem):
    me = lax.axis_index("cuts")
    slices, rows, width = stem_hbm.shape[1], stem_hbm.shape[2], stem_hbm.shape[3]
    mine = out_ref.shape[1] - LANES
    lines = mine // LANES

    cols_load = pltpu.make_async_copy(cols_hbm, cols_v, load_sems.at[0])
    rows_load = pltpu.make_async_copy(rows_hbm, rows_v, load_sems.at[1])
    cut_load = pltpu.make_async_copy(cut_hbm, cut_s, load_sems.at[2])
    stem_load = pltpu.make_async_copy(stem_hbm, stem_v, load_sems.at[3])
    branch_loads = [
        [
            pltpu.make_async_copy(
                branch_hbm.at[step, value, part], held.at[value, part], load_sems.at[4 + 4 * step + 2 * value + part])
            for value in range(2) for part in range(2)
        ]
        for step, held in enumerate((early_v, later_v))
    ]
    for load in [cols_load, stem_load, cut_load] + branch_loads[0] + [rows_load] + branch_loads[1]:
        load.start()

    barrier = pltpu.get_barrier_semaphore()

    def greet(k, carry):
        pl.semaphore_signal(barrier, inc=1, device_id={"cuts": lax.rem(me + k, n)}, device_id_type=pl.DeviceIdType.MESH)
        return carry

    lax.fori_loop(1, n, greet, 0)

    def hot_columns(dest):
        col_lines = cols_v[dest]
        column = lax.broadcasted_iota(jnp.int16, (LANES, LANES), 0)
        one, zero = jnp.bfloat16(1), jnp.bfloat16(0)
        low_part = lax.rem(col_lines, LANES)
        lanes = [jnp.broadcast_to(low_part[j:j + 1], (LANES, LANES)).astype(jnp.int16) for j in range(lines)]
        return jnp.concatenate([jnp.where(column == line, one, zero) for line in lanes], axis=1)

    def nth_dest(i):
        swing = (i + 1) // 2
        return lax.rem(me + n // 2 + swing * (1 - 2 * (i % 2)) + n, n)

    def keep_hot(i, carry):
        hot_v[i] = hot_columns(nth_dest(i))
        return carry

    cols_load.wait()
    if hot_v.shape[0] == n:
        lax.fori_loop(0, n, keep_hot, 0)

    cut_load.wait()
    stem_load.wait()
    for load in branch_loads[0]:
        load.wait()
    first = []
    for s in range(slices):
        weights = early_v[cut_s[0, s]].reshape(2 * width, width)
        first.append(complex_step(stem_v[0, s], stem_v[1, s], weights))
    for load in branch_loads[1]:
        load.wait()
    second = []
    for s in range(slices):
        state = (first[s] * LIFT).astype(jnp.bfloat16)
        weights = later_v[cut_s[1, s]].reshape(2 * width, width)
        second.append(complex_step(state[:rows], state[rows:], weights))

    square = functools.reduce(jnp.maximum, [p[:rows] * p[:rows] + p[rows:] * p[rows:] for p in first])
    peak_square = largest(square)
    own_peak = jnp.sqrt(peak_square) + 1e-06
    shrink = (1.0 / LIFT) / own_peak
    shrunk = [p * shrink for p in second]
    square = functools.reduce(jnp.maximum, [p[:rows] * p[:rows] + p[rows:] * p[rows:] for p in shrunk])
    raw_second = jnp.sqrt(largest(square)) * own_peak
    stats = jnp.concatenate(
        [jnp.broadcast_to(peak_square, (1, LANES)), jnp.broadcast_to(raw_second, (1, LANES))], axis=0)

    table = functools.reduce(jnp.add, second)
    high = table.astype(jnp.bfloat16)
    low = (table - high.astype(jnp.float32)).astype(jnp.bfloat16)
    blocks = width // LANES

    def blocked(half):
        return jnp.concatenate(
            [half[p * rows:(p + 1) * rows, c * LANES:(c + 1) * LANES] for p in range(2) for c in range(blocks)], axis=0)

    left = jnp.concatenate([blocked(high), blocked(low)], axis=1)

    rows_load.wait()
    pl.semaphore_wait(barrier, n - 1)

    def picked(dest, hot):
        spots = blocks * rows
        spot_lines = (cols_v[dest] // LANES) * rows + rows_v[dest]
        spot = lax.broadcasted_iota(jnp.int32, (spots, LANES), 0)
        found = jnp.dot(left, jnp.concatenate([hot, hot], axis=0), preferred_element_type=jnp.float32)
        chosen = jnp.concatenate([spot == spot_lines[j:j + 1] for j in range(lines)], axis=1)
        parts = [jnp.sum(jnp.where(chosen, found[p * spots:(p + 1) * spots], 0.0), axis=0, keepdims=True) for p in range(2)]
        return jnp.concatenate(parts, axis=0)

    def remote(dest):
        return pltpu.make_async_remote_copy(
            src_ref=outgoing.at[dest],
            dst_ref=incoming.at[me],
            send_sem=send_sem,
            recv_sem=recv_sem,
            device_id={"cuts": dest},
            device_id_type=pl.DeviceIdType.MESH,
        )

    def serve(start, count):
        dests = [nth_dest(start + i) for i in range(count)]
        for i, dest in enumerate(dests):
            hot = hot_v[start + i] if hot_v.shape[0] == n else hot_columns(dest)
            outgoing[dest, :, :mine] = picked(dest, hot)
            outgoing[dest, :, mine:] = stats
        for dest in dests:
            remote(dest).start()

    def serve_group(g, carry):
        serve(g * group, group)
        return carry

    rounds = (n - 1) // group
    if hot_v.shape[0] == n:
        for g in range(rounds):
            serve(g * group, group)
    else:
        lax.fori_loop(0, rounds, serve_group, 0)
    serve(rounds * group, n - 1 - rounds * group)
    incoming[me, :, :mine] = picked(me, hot_v[n - 1] if hot_v.shape[0] == n else hot_columns(me))
    incoming[me, :, mine:] = stats

    everything = pl.ds(0, n - 1)
    pltpu.make_async_copy(outgoing.at[everything], incoming.at[everything], recv_sem).wait()
    pltpu.make_async_copy(outgoing.at[everything], incoming.at[everything], send_sem).wait()
    out_ref[:, :mine] = jnp.sum(incoming[:, :, :mine], axis=0)
    out_ref[:, mine:] = jnp.max(incoming[:, :, mine:], axis=0)


def finish(sum_ref, amp_hbm, log_hbm, amp_v, log_v, sems):
    mine = amp_v.shape[1]
    peaks = sum_ref[:, mine:]
    first_peak = jnp.sqrt(peaks[0:1, 0:1]) + 1e-06
    second_peak = peaks[1:2, 0:1] / first_peak + 1e-06
    log_v[...] = jnp.log(first_peak) + jnp.log(second_peak)
    log_store = pltpu.make_async_copy(log_v, log_hbm, sems.at[0])
    log_store.start()
    amp_v[...] = sum_ref[:, :mine] * ((1.0 / LIFT) / first_peak) / second_peak
    amp_store = pltpu.make_async_copy(amp_v, amp_hbm, sems.at[1])
    amp_store.start()
    log_store.wait()
    amp_store.wait()


def shards(stem_tensor, branch_tensors, cut_values, bit_rows, bit_cols):
    n = lax.axis_size("cuts")
    slices = stem_tensor.shape[1]
    mine = bit_rows.shape[0] // n
    steps = branch_tensors.shape[0]
    any_spec = pl.BlockSpec(memory_space=pl.ANY)
    lined = (n, mine // LANES, LANES)
    sums = pl.pallas_call(
        functools.partial(kernel, n, 3),
        out_shape=pltpu.VMEM((2, mine + LANES), jnp.float32),
        in_specs=[any_spec] * 5,
        out_specs=pl.BlockSpec(memory_space=pltpu.VMEM),
        scratch_shapes=[
            pltpu.SMEM((steps, slices), jnp.int32),
            pltpu.VMEM(stem_tensor.shape, jnp.bfloat16),
            pltpu.VMEM(branch_tensors.shape[1:], jnp.bfloat16),
            pltpu.VMEM(branch_tensors.shape[1:], jnp.bfloat16),
            pltpu.VMEM(lined, jnp.int32),
            pltpu.VMEM(lined, jnp.int32),
            pltpu.VMEM((n if n <= 16 else 1, LANES, mine), jnp.bfloat16),
            pltpu.VMEM((n, 2, mine + LANES), jnp.float32),
            pltpu.VMEM((n, 2, mine + LANES), jnp.float32),
            pltpu.SemaphoreType.DMA((4 + 4 * steps,)),
            pltpu.SemaphoreType.DMA,
            pltpu.SemaphoreType.DMA,
        ],
        compiler_params=pltpu.CompilerParams(
            collective_id=0, has_side_effects=True, vmem_limit_bytes=56 * 1024 * 1024
        ),
    )(cut_values.T, stem_tensor, branch_tensors, bit_rows.reshape(lined), bit_cols.reshape(lined))
    amplitudes, log_scale = pl.pallas_call(
        finish,
        out_shape=(
            jax.ShapeDtypeStruct((2, mine), jnp.float32),
            jax.ShapeDtypeStruct((1, 1), jnp.float32),
        ),
        in_specs=[pl.BlockSpec(memory_space=pltpu.VMEM)],
        out_specs=(any_spec, any_spec),
        scratch_shapes=[
            pltpu.VMEM((2, mine), jnp.float32),
            pltpu.VMEM((1, 1), jnp.float32),
            pltpu.SemaphoreType.DMA((2,)),
        ],
    )(pltpu.with_memory_space_constraint(sums, pltpu.VMEM))
    return (amplitudes, log_scale.reshape(1))


def solution(mesh):
    placed = (
        P(None, ("grp", "cuts"), None, None),
        P(),
        P(("grp", "cuts"), None),
        P("grp"),
        P("grp"),
    )
    return jax.shard_map(
        shards,
        mesh=mesh,
        in_specs=placed,
        out_specs=(P(None, ("grp", "cuts")), P("grp")),
        check_vma=False,
    )
```

```python
import functools

import jax
import jax.numpy as jnp
from jax import lax
from jax.experimental import pallas as pl
from jax.experimental.pallas import tpu as pltpu
from jax.sharding import PartitionSpec as P

LANES = 128
LIFT = 2.0 ** 20


def complex_step(real_part, imag_part, weights):
    upper = jnp.concatenate([real_part, -imag_part], axis=1)
    lower = jnp.concatenate([imag_part, real_part], axis=1)
    left = jnp.concatenate([upper, lower], axis=0)
    return jnp.dot(left, weights, preferred_element_type=jnp.float32)


def largest(values):
    return jnp.max(jnp.max(values, axis=0, keepdims=True), axis=1, keepdims=True)


def kernel(n, group, cut_hbm, stem_hbm, branch_hbm, rows_hbm, cols_hbm, out_ref,
           cut_s, stem_v, early_v, later_v, rows_v, cols_v, hot_v, outgoing, incoming, load_sems, send_sem, recv_sem):
    me = lax.axis_index("cuts")
    slices, rows, width = stem_hbm.shape[1], stem_hbm.shape[2], stem_hbm.shape[3]
    mine = out_ref.shape[1] - LANES
    lines = mine // LANES

    cols_load = pltpu.make_async_copy(cols_hbm, cols_v, load_sems.at[0])
    rows_load = pltpu.make_async_copy(rows_hbm, rows_v, load_sems.at[1])
    cut_load = pltpu.make_async_copy(cut_hbm, cut_s, load_sems.at[2])
    stem_load = pltpu.make_async_copy(stem_hbm, stem_v, load_sems.at[3])
    branch_loads = [
        [
            pltpu.make_async_copy(
                branch_hbm.at[step, value, part], held.at[value, part], load_sems.at[4 + 4 * step + 2 * value + part])
            for value in range(2) for part in range(2)
        ]
        for step, held in enumerate((early_v, later_v))
    ]
    for load in [cols_load, stem_load, cut_load] + branch_loads[0] + [rows_load] + branch_loads[1]:
        load.start()

    barrier = pltpu.get_barrier_semaphore()

    def greet(k, carry):
        pl.semaphore_signal(barrier, inc=1, device_id={"cuts": lax.rem(me + k, n)}, device_id_type=pl.DeviceIdType.MESH)
        return carry

    lax.fori_loop(1, n, greet, 0)

    def hot_columns(dest):
        col_lines = cols_v[dest]
        column = lax.broadcasted_iota(jnp.int16, (LANES, LANES), 0)
        one, zero = jnp.bfloat16(1), jnp.bfloat16(0)
        low_part = lax.rem(col_lines, LANES)
        lanes = [jnp.broadcast_to(low_part[j:j + 1], (LANES, LANES)).astype(jnp.int16) for j in range(lines)]
        return jnp.concatenate([jnp.where(column == line, one, zero) for line in lanes], axis=1)

    def nth_dest(i):
        return jnp.where(i >= n - 1, me, jnp.where(i >= me, i + 1, i))

    def keep_hot(i, carry):
        hot_v[i] = hot_columns(nth_dest(i))
        return carry

    cols_load.wait()
    if hot_v.shape[0] == n:
        lax.fori_loop(0, n, keep_hot, 0)

    cut_load.wait()
    stem_load.wait()
    for load in branch_loads[0]:
        load.wait()
    first = []
    for s in range(slices):
        weights = early_v[cut_s[0, s]].reshape(2 * width, width)
        first.append(complex_step(stem_v[0, s], stem_v[1, s], weights))
    for load in branch_loads[1]:
        load.wait()
    second = []
    for s in range(slices):
        state = (first[s] * LIFT).astype(jnp.bfloat16)
        weights = later_v[cut_s[1, s]].reshape(2 * width, width)
        second.append(complex_step(state[:rows], state[rows:], weights))

    square = functools.reduce(jnp.maximum, [p[:rows] * p[:rows] + p[rows:] * p[rows:] for p in first])
    peak_square = largest(square)
    own_peak = jnp.sqrt(peak_square) + 1e-06
    shrink = (1.0 / LIFT) / own_peak
    shrunk = [p * shrink for p in second]
    square = functools.reduce(jnp.maximum, [p[:rows] * p[:rows] + p[rows:] * p[rows:] for p in shrunk])
    raw_second = jnp.sqrt(largest(square)) * own_peak
    stats = jnp.concatenate(
        [jnp.broadcast_to(peak_square, (1, LANES)), jnp.broadcast_to(raw_second, (1, LANES))], axis=0)

    table = functools.reduce(jnp.add, second)
    high = table.astype(jnp.bfloat16)
    low = (table - high.astype(jnp.float32)).astype(jnp.bfloat16)
    blocks = width // LANES

    def blocked(half):
        return jnp.concatenate(
            [half[p * rows:(p + 1) * rows, c * LANES:(c + 1) * LANES] for p in range(2) for c in range(blocks)], axis=0)

    left = jnp.concatenate([blocked(high), blocked(low)], axis=1)

    rows_load.wait()
    pl.semaphore_wait(barrier, n - 1)

    def picked(dest, hot):
        spots = blocks * rows
        spot_lines = (cols_v[dest] // LANES) * rows + rows_v[dest]
        spot = lax.broadcasted_iota(jnp.int32, (spots, LANES), 0)
        found = jnp.dot(left, jnp.concatenate([hot, hot], axis=0), preferred_element_type=jnp.float32)
        chosen = jnp.concatenate([spot == spot_lines[j:j + 1] for j in range(lines)], axis=1)
        parts = [jnp.sum(jnp.where(chosen, found[p * spots:(p + 1) * spots], 0.0), axis=0, keepdims=True) for p in range(2)]
        return jnp.concatenate(parts, axis=0)

    def remote(dest):
        return pltpu.make_async_remote_copy(
            src_ref=outgoing.at[dest],
            dst_ref=incoming.at[me],
            send_sem=send_sem,
            recv_sem=recv_sem,
            device_id={"cuts": dest},
            device_id_type=pl.DeviceIdType.MESH,
        )

    def serve(start, count):
        dests = [nth_dest(start + i) for i in range(count)]
        for i, dest in enumerate(dests):
            hot = hot_v[start + i] if hot_v.shape[0] == n else hot_columns(dest)
            outgoing[dest, :, :mine] = picked(dest, hot)
            outgoing[dest, :, mine:] = stats
        for dest in dests:
            remote(dest).start()

    def serve_group(g, carry):
        serve(g * group, group)
        return carry

    rounds = (n - 1) // group
    if hot_v.shape[0] == n:
        for g in range(rounds):
            serve(g * group, group)
    else:
        lax.fori_loop(0, rounds, serve_group, 0)
    serve(rounds * group, n - 1 - rounds * group)
    incoming[me, :, :mine] = picked(me, hot_v[n - 1] if hot_v.shape[0] == n else hot_columns(me))
    incoming[me, :, mine:] = stats

    everything = pl.ds(0, n - 1)
    pltpu.make_async_copy(outgoing.at[everything], incoming.at[everything], recv_sem).wait()
    pltpu.make_async_copy(outgoing.at[everything], incoming.at[everything], send_sem).wait()
    out_ref[:, :mine] = jnp.sum(incoming[:, :, :mine], axis=0)
    out_ref[:, mine:] = jnp.max(incoming[:, :, mine:], axis=0)


def finish(sum_ref, amp_hbm, log_hbm, amp_v, log_v, sems):
    mine = amp_v.shape[1]
    peaks = sum_ref[:, mine:]
    first_peak = jnp.sqrt(peaks[0:1, 0:1]) + 1e-06
    second_peak = peaks[1:2, 0:1] / first_peak + 1e-06
    log_v[...] = jnp.log(first_peak) + jnp.log(second_peak)
    log_store = pltpu.make_async_copy(log_v, log_hbm, sems.at[0])
    log_store.start()
    amp_v[...] = sum_ref[:, :mine] * ((1.0 / LIFT) / first_peak) / second_peak
    amp_store = pltpu.make_async_copy(amp_v, amp_hbm, sems.at[1])
    amp_store.start()
    log_store.wait()
    amp_store.wait()


def shards(stem_tensor, branch_tensors, cut_values, bit_rows, bit_cols):
    n = lax.axis_size("cuts")
    slices = stem_tensor.shape[1]
    mine = bit_rows.shape[0] // n
    steps = branch_tensors.shape[0]
    any_spec = pl.BlockSpec(memory_space=pl.ANY)
    lined = (n, mine // LANES, LANES)
    sums = pl.pallas_call(
        functools.partial(kernel, n, 2),
        out_shape=pltpu.VMEM((2, mine + LANES), jnp.float32),
        in_specs=[any_spec] * 5,
        out_specs=pl.BlockSpec(memory_space=pltpu.VMEM),
        scratch_shapes=[
            pltpu.SMEM((steps, slices), jnp.int32),
            pltpu.VMEM(stem_tensor.shape, jnp.bfloat16),
            pltpu.VMEM(branch_tensors.shape[1:], jnp.bfloat16),
            pltpu.VMEM(branch_tensors.shape[1:], jnp.bfloat16),
            pltpu.VMEM(lined, jnp.int32),
            pltpu.VMEM(lined, jnp.int32),
            pltpu.VMEM((n if n <= 16 else 1, LANES, mine), jnp.bfloat16),
            pltpu.VMEM((n, 2, mine + LANES), jnp.float32),
            pltpu.VMEM((n, 2, mine + LANES), jnp.float32),
            pltpu.SemaphoreType.DMA((4 + 4 * steps,)),
            pltpu.SemaphoreType.DMA,
            pltpu.SemaphoreType.DMA,
        ],
        compiler_params=pltpu.CompilerParams(
            collective_id=0, has_side_effects=True, vmem_limit_bytes=56 * 1024 * 1024
        ),
    )(cut_values.T, stem_tensor, branch_tensors, bit_rows.reshape(lined), bit_cols.reshape(lined))
    amplitudes, log_scale = pl.pallas_call(
        finish,
        out_shape=(
            jax.ShapeDtypeStruct((2, mine), jnp.float32),
            jax.ShapeDtypeStruct((1, 1), jnp.float32),
        ),
        in_specs=[pl.BlockSpec(memory_space=pltpu.VMEM)],
        out_specs=(any_spec, any_spec),
        scratch_shapes=[
            pltpu.VMEM((2, mine), jnp.float32),
            pltpu.VMEM((1, 1), jnp.float32),
            pltpu.SemaphoreType.DMA((2,)),
        ],
    )(pltpu.with_memory_space_constraint(sums, pltpu.VMEM))
    return (amplitudes, log_scale.reshape(1))


def solution(mesh):
    placed = (
        P(None, ("grp", "cuts"), None, None),
        P(),
        P(("grp", "cuts"), None),
        P("grp"),
        P("grp"),
    )
    return jax.shard_map(
        shards,
        mesh=mesh,
        in_specs=placed,
        out_specs=(P(None, ("grp", "cuts")), P("grp")),
        check_vma=False,
    )
```

```python
import functools

import jax
import jax.numpy as jnp
from jax import lax
from jax.experimental import pallas as pl
from jax.experimental.pallas import tpu as pltpu
from jax.sharding import PartitionSpec as P

LANES = 128
LIFT = 2.0 ** 20


def complex_step(parts, flags, matrices):
    rows = []
    for (real_part, imag_part), flag in zip(parts, flags):
        real_parts = [real_part * f for f in flag]
        imag_parts = [imag_part * f for f in flag]
        for signed in ([[r, -i] for r, i in zip(real_parts, imag_parts)], [[i, r] for r, i in zip(real_parts, imag_parts)]):
            rows.append(jnp.concatenate([x.astype(jnp.bfloat16) for pair in signed for x in pair], axis=1))
    left = jnp.concatenate(rows, axis=0)
    values, kinds, depth, width = matrices.shape
    found = jnp.dot(left, matrices.reshape(values * kinds * depth, width), preferred_element_type=jnp.float32)
    height = found.shape[0] // len(parts)
    return [found[s * height:(s + 1) * height] for s in range(len(parts))]


def largest(values):
    return jnp.max(jnp.max(values, axis=0, keepdims=True), axis=1, keepdims=True)


def kernel(n, group, cut_hbm, stem_hbm, branch_hbm, rows_hbm, cols_hbm, out_ref,
           cut_s, stem_v, early_v, later_v, rows_v, cols_v, hot_v, outgoing, incoming, load_sems, send_sem, recv_sem):
    me = lax.axis_index("cuts")
    slices, rows, width = stem_hbm.shape[1], stem_hbm.shape[2], stem_hbm.shape[3]
    mine = out_ref.shape[1] - LANES
    lines = mine // LANES

    cols_load = pltpu.make_async_copy(cols_hbm, cols_v, load_sems.at[0])
    rows_load = pltpu.make_async_copy(rows_hbm, rows_v, load_sems.at[1])
    cut_load = pltpu.make_async_copy(cut_hbm, cut_s, load_sems.at[2])
    stem_load = pltpu.make_async_copy(stem_hbm, stem_v, load_sems.at[3])
    branch_loads = [
        [
            pltpu.make_async_copy(
                branch_hbm.at[step, value, part], held.at[value, part], load_sems.at[4 + 4 * step + 2 * value + part])
            for value in range(2) for part in range(2)
        ]
        for step, held in enumerate((early_v, later_v))
    ]
    for load in [cols_load, stem_load, cut_load] + branch_loads[0] + [rows_load] + branch_loads[1]:
        load.start()

    barrier = pltpu.get_barrier_semaphore()

    def greet(k, carry):
        pl.semaphore_signal(barrier, inc=1, device_id={"cuts": lax.rem(me + k, n)}, device_id_type=pl.DeviceIdType.MESH)
        return carry

    lax.fori_loop(1, n, greet, 0)

    def hot_columns(dest):
        col_lines = cols_v[dest]
        column = lax.broadcasted_iota(jnp.int16, (LANES, LANES), 0)
        one, zero = jnp.bfloat16(1), jnp.bfloat16(0)
        low_part = lax.rem(col_lines, LANES)
        lanes = [jnp.broadcast_to(low_part[j:j + 1], (LANES, LANES)).astype(jnp.int16) for j in range(lines)]
        return jnp.concatenate([jnp.where(column == line, one, zero) for line in lanes], axis=1)

    def nth_dest(i):
        return jnp.where(i >= n - 1, me, jnp.where(i >= me, i + 1, i))

    def keep_hot(i, carry):
        hot_v[i] = hot_columns(nth_dest(i))
        return carry

    cols_load.wait()
    if hot_v.shape[0] == n:
        lax.fori_loop(0, n, keep_hot, 0)

    cut_load.wait()
    stem_load.wait()
    for load in branch_loads[0]:
        load.wait()
    def flags(step, scale, dtype):
        return [
            [jnp.full((1, 1), jnp.where(cut_s[step, s] == v, scale, 0.0)).astype(dtype) for v in range(2)]
            for s in range(slices)
        ]

    first = complex_step(
        [(stem_v[0, s], stem_v[1, s]) for s in range(slices)], flags(0, 1.0, jnp.bfloat16), early_v[...])
    for load in branch_loads[1]:
        load.wait()
    second = complex_step([(p[:rows], p[rows:]) for p in first], flags(1, LIFT, jnp.float32), later_v[...])

    square = functools.reduce(jnp.maximum, [p[:rows] * p[:rows] + p[rows:] * p[rows:] for p in first])
    peak_square = largest(square)
    own_peak = jnp.sqrt(peak_square) + 1e-06
    shrink = (1.0 / LIFT) / own_peak
    shrunk = [p * shrink for p in second]
    square = functools.reduce(jnp.maximum, [p[:rows] * p[:rows] + p[rows:] * p[rows:] for p in shrunk])
    raw_second = jnp.sqrt(largest(square)) * own_peak
    stats = jnp.concatenate(
        [jnp.broadcast_to(peak_square, (1, LANES)), jnp.broadcast_to(raw_second, (1, LANES))], axis=0)

    table = functools.reduce(jnp.add, second)
    high = table.astype(jnp.bfloat16)
    low = (table - high.astype(jnp.float32)).astype(jnp.bfloat16)
    blocks = width // LANES

    def blocked(half):
        return jnp.concatenate(
            [half[p * rows:(p + 1) * rows, c * LANES:(c + 1) * LANES] for p in range(2) for c in range(blocks)], axis=0)

    left = jnp.concatenate([blocked(high), blocked(low)], axis=1)

    rows_load.wait()
    pl.semaphore_wait(barrier, n - 1)

    def picked(dest, hot):
        spots = blocks * rows
        spot_lines = (cols_v[dest] // LANES) * rows + rows_v[dest]
        spot = lax.broadcasted_iota(jnp.int32, (spots, LANES), 0)
        found = jnp.dot(left, jnp.concatenate([hot, hot], axis=0), preferred_element_type=jnp.float32)
        chosen = jnp.concatenate([spot == spot_lines[j:j + 1] for j in range(lines)], axis=1)
        parts = [jnp.sum(jnp.where(chosen, found[p * spots:(p + 1) * spots], 0.0), axis=0, keepdims=True) for p in range(2)]
        return jnp.concatenate(parts, axis=0)

    def remote(dest):
        return pltpu.make_async_remote_copy(
            src_ref=outgoing.at[dest],
            dst_ref=incoming.at[me],
            send_sem=send_sem,
            recv_sem=recv_sem,
            device_id={"cuts": dest},
            device_id_type=pl.DeviceIdType.MESH,
        )

    def serve(start, count):
        dests = [nth_dest(start + i) for i in range(count)]
        for i, dest in enumerate(dests):
            hot = hot_v[start + i] if hot_v.shape[0] == n else hot_columns(dest)
            outgoing[dest, :, :mine] = picked(dest, hot)
            outgoing[dest, :, mine:] = stats
        for dest in dests:
            remote(dest).start()

    def serve_group(g, carry):
        serve(g * group, group)
        return carry

    rounds = (n - 1) // group
    if hot_v.shape[0] == n:
        for g in range(rounds):
            serve(g * group, group)
    else:
        lax.fori_loop(0, rounds, serve_group, 0)
    serve(rounds * group, n - 1 - rounds * group)
    incoming[me, :, :mine] = picked(me, hot_v[n - 1] if hot_v.shape[0] == n else hot_columns(me))
    incoming[me, :, mine:] = stats

    everything = pl.ds(0, n - 1)
    pltpu.make_async_copy(outgoing.at[everything], incoming.at[everything], recv_sem).wait()
    pltpu.make_async_copy(outgoing.at[everything], incoming.at[everything], send_sem).wait()
    out_ref[:, :mine] = jnp.sum(incoming[:, :, :mine], axis=0)
    out_ref[:, mine:] = jnp.max(incoming[:, :, mine:], axis=0)


def finish(sum_ref, amp_hbm, log_hbm, amp_v, log_v, sems):
    mine = amp_v.shape[1]
    peaks = sum_ref[:, mine:]
    first_peak = jnp.sqrt(peaks[0:1, 0:1]) + 1e-06
    second_peak = peaks[1:2, 0:1] / first_peak + 1e-06
    log_v[...] = jnp.log(first_peak) + jnp.log(second_peak)
    log_store = pltpu.make_async_copy(log_v, log_hbm, sems.at[0])
    log_store.start()
    amp_v[...] = sum_ref[:, :mine] * ((1.0 / LIFT) / first_peak) / second_peak
    amp_store = pltpu.make_async_copy(amp_v, amp_hbm, sems.at[1])
    amp_store.start()
    log_store.wait()
    amp_store.wait()


def shards(stem_tensor, branch_tensors, cut_values, bit_rows, bit_cols):
    n = lax.axis_size("cuts")
    slices = stem_tensor.shape[1]
    mine = bit_rows.shape[0] // n
    steps = branch_tensors.shape[0]
    any_spec = pl.BlockSpec(memory_space=pl.ANY)
    lined = (n, mine // LANES, LANES)
    sums = pl.pallas_call(
        functools.partial(kernel, n, 2),
        out_shape=pltpu.VMEM((2, mine + LANES), jnp.float32),
        in_specs=[any_spec] * 5,
        out_specs=pl.BlockSpec(memory_space=pltpu.VMEM),
        scratch_shapes=[
            pltpu.SMEM((steps, slices), jnp.int32),
            pltpu.VMEM(stem_tensor.shape, jnp.bfloat16),
            pltpu.VMEM(branch_tensors.shape[1:], jnp.bfloat16),
            pltpu.VMEM(branch_tensors.shape[1:], jnp.bfloat16),
            pltpu.VMEM(lined, jnp.int32),
            pltpu.VMEM(lined, jnp.int32),
            pltpu.VMEM((n if n <= 16 else 1, LANES, mine), jnp.bfloat16),
            pltpu.VMEM((n, 2, mine + LANES), jnp.float32),
            pltpu.VMEM((n, 2, mine + LANES), jnp.float32),
            pltpu.SemaphoreType.DMA((4 + 4 * steps,)),
            pltpu.SemaphoreType.DMA,
            pltpu.SemaphoreType.DMA,
        ],
        compiler_params=pltpu.CompilerParams(
            collective_id=0, has_side_effects=True, vmem_limit_bytes=56 * 1024 * 1024
        ),
    )(cut_values.T, stem_tensor, branch_tensors, bit_rows.reshape(lined), bit_cols.reshape(lined))
    amplitudes, log_scale = pl.pallas_call(
        finish,
        out_shape=(
            jax.ShapeDtypeStruct((2, mine), jnp.float32),
            jax.ShapeDtypeStruct((1, 1), jnp.float32),
        ),
        in_specs=[pl.BlockSpec(memory_space=pltpu.VMEM)],
        out_specs=(any_spec, any_spec),
        scratch_shapes=[
            pltpu.VMEM((2, mine), jnp.float32),
            pltpu.VMEM((1, 1), jnp.float32),
            pltpu.SemaphoreType.DMA((2,)),
        ],
    )(pltpu.with_memory_space_constraint(sums, pltpu.VMEM))
    return (amplitudes, log_scale.reshape(1))


def solution(mesh):
    placed = (
        P(None, ("grp", "cuts"), None, None),
        P(),
        P(("grp", "cuts"), None),
        P("grp"),
        P("grp"),
    )
    return jax.shard_map(
        shards,
        mesh=mesh,
        in_specs=placed,
        out_specs=(P(None, ("grp", "cuts")), P("grp")),
        check_vma=False,
    )
```

```python
import functools

import jax
import jax.numpy as jnp
from jax import lax
from jax.experimental import pallas as pl
from jax.experimental.pallas import tpu as pltpu
from jax.sharding import PartitionSpec as P

LANES = 128
LIFT = 2.0 ** 20


def complex_step(parts, flags, matrices, loads):
    found = None
    for v in range(matrices.shape[0]):
        rows = []
        for (real_part, imag_part), flag in zip(parts, flags):
            real_now = real_part * flag[v]
            imag_now = imag_part * flag[v]
            for pair in ((real_now, -imag_now), (imag_now, real_now)):
                rows.append(jnp.concatenate([x.astype(jnp.bfloat16) for x in pair], axis=1))
        left = jnp.concatenate(rows, axis=0)
        for load in loads[v]:
            load.wait()
        _, kinds, depth, width = matrices.shape
        product = jnp.dot(left, matrices[v].reshape(kinds * depth, width), preferred_element_type=jnp.float32)
        found = product if found is None else found + product
    height = found.shape[0] // len(parts)
    return [found[s * height:(s + 1) * height] for s in range(len(parts))]


def largest(values):
    return jnp.max(jnp.max(values, axis=0, keepdims=True), axis=1, keepdims=True)


def kernel(n, group, cut_hbm, stem_hbm, branch_hbm, rows_hbm, cols_hbm, out_ref,
           cut_s, stem_v, early_v, later_v, rows_v, cols_v, outgoing, incoming, load_sems, send_sem, recv_sem):
    me = lax.axis_index("cuts")
    slices, rows, width = stem_hbm.shape[1], stem_hbm.shape[2], stem_hbm.shape[3]
    mine = out_ref.shape[1] - LANES
    lines = mine // LANES

    cols_load = pltpu.make_async_copy(cols_hbm, cols_v, load_sems.at[0])
    rows_load = pltpu.make_async_copy(rows_hbm, rows_v, load_sems.at[1])
    cut_load = pltpu.make_async_copy(cut_hbm, cut_s, load_sems.at[2])
    stem_load = pltpu.make_async_copy(stem_hbm, stem_v, load_sems.at[3])
    branch_loads = [
        [
            [
                pltpu.make_async_copy(
                    branch_hbm.at[step, value, part], held.at[value, part], load_sems.at[4 + 4 * step + 2 * value + part])
                for part in range(2)
            ]
            for value in range(2)
        ]
        for step, held in enumerate((early_v, later_v))
    ]
    for load in [cut_load, stem_load, *branch_loads[0][0], *branch_loads[0][1], cols_load, rows_load,
                 *branch_loads[1][0], *branch_loads[1][1]]:
        load.start()

    barrier = pltpu.get_barrier_semaphore()

    def greet(k, carry):
        pl.semaphore_signal(barrier, inc=1, device_id={"cuts": lax.rem(me + k, n)}, device_id_type=pl.DeviceIdType.MESH)
        return carry

    lax.fori_loop(1, n, greet, 0)

    def hot_columns(dest):
        col_lines = cols_v[dest]
        column = lax.broadcasted_iota(jnp.int16, (LANES, LANES), 0)
        one, zero = jnp.bfloat16(1), jnp.bfloat16(0)
        low_part = lax.rem(col_lines, LANES)
        lanes = [jnp.broadcast_to(low_part[j:j + 1], (LANES, LANES)).astype(jnp.int16) for j in range(lines)]
        return jnp.concatenate([jnp.where(column == line, one, zero) for line in lanes], axis=1)

    def nth_dest(i):
        return jnp.where(i >= n - 1, me, jnp.where(i >= me, i + 1, i))

    cut_load.wait()
    stem_load.wait()
    def flags(step, scale, dtype):
        return [
            [jnp.full((1, 1), jnp.where(cut_s[step, s] == v, scale, 0.0)).astype(dtype) for v in range(2)]
            for s in range(slices)
        ]

    first = complex_step(
        [(stem_v[0, s], stem_v[1, s]) for s in range(slices)], flags(0, 1.0, jnp.bfloat16), early_v, branch_loads[0])
    cols_load.wait()
    rows_load.wait()
    for load in branch_loads[1][0] + branch_loads[1][1]:
        load.wait()
    second = complex_step([(p[:rows], p[rows:]) for p in first], flags(1, LIFT, jnp.float32), later_v, [[], []])

    square = functools.reduce(jnp.maximum, [p[:rows] * p[:rows] + p[rows:] * p[rows:] for p in first])
    peak_square = largest(square)
    own_peak = jnp.sqrt(peak_square) + 1e-06
    shrink = (1.0 / LIFT) / own_peak
    shrunk = [p * shrink for p in second]
    square = functools.reduce(jnp.maximum, [p[:rows] * p[:rows] + p[rows:] * p[rows:] for p in shrunk])
    raw_second = jnp.sqrt(largest(square)) * own_peak
    stats = jnp.concatenate(
        [jnp.broadcast_to(peak_square, (1, LANES)), jnp.broadcast_to(raw_second, (1, LANES))], axis=0)

    table = functools.reduce(jnp.add, second)
    high = table.astype(jnp.bfloat16)
    low = (table - high.astype(jnp.float32)).astype(jnp.bfloat16)
    blocks = width // LANES

    def blocked(half):
        return jnp.concatenate(
            [half[p * rows:(p + 1) * rows, c * LANES:(c + 1) * LANES] for p in range(2) for c in range(blocks)], axis=0)

    left = jnp.concatenate([blocked(high), blocked(low)], axis=1)

    def picked(dest):
        hot = hot_columns(dest)
        spots = blocks * rows
        spot_lines = (cols_v[dest] // LANES) * rows + rows_v[dest]
        spot = lax.broadcasted_iota(jnp.int32, (spots, LANES), 0)
        found = jnp.dot(left, jnp.concatenate([hot, hot], axis=0), preferred_element_type=jnp.float32)
        chosen = jnp.concatenate([spot == spot_lines[j:j + 1] for j in range(lines)], axis=1)
        parts = [jnp.sum(jnp.where(chosen, found[p * spots:(p + 1) * spots], 0.0), axis=0, keepdims=True) for p in range(2)]
        return jnp.concatenate(parts, axis=0)

    def remote(dest):
        return pltpu.make_async_remote_copy(
            src_ref=outgoing.at[dest],
            dst_ref=incoming.at[me],
            send_sem=send_sem,
            recv_sem=recv_sem,
            device_id={"cuts": dest},
            device_id_type=pl.DeviceIdType.MESH,
        )

    def serve(start, count):
        dests = [nth_dest(start + i) for i in range(count)]
        for dest in dests:
            outgoing[dest, :, :mine] = picked(dest)
            outgoing[dest, :, mine:] = stats
        if isinstance(start, int) and start == 0:
            pl.semaphore_wait(barrier, n - 1)
        for dest in dests:
            remote(dest).start()

    def serve_group(g, carry):
        serve(g * group, group)
        return carry

    serve(0, group)
    rounds = (n - 1) // group
    if n <= 16:
        for g in range(1, rounds):
            serve(g * group, group)
    else:
        lax.fori_loop(1, rounds, serve_group, 0)
    serve(rounds * group, n - 1 - rounds * group)
    incoming[me, :, :mine] = picked(me)
    incoming[me, :, mine:] = stats

    everything = pl.ds(0, n - 1)
    pltpu.make_async_copy(outgoing.at[everything], incoming.at[everything], recv_sem).wait()
    pltpu.make_async_copy(outgoing.at[everything], incoming.at[everything], send_sem).wait()
    out_ref[:, :mine] = jnp.sum(incoming[:, :, :mine], axis=0)
    out_ref[:, mine:] = jnp.max(incoming[:, :, mine:], axis=0)


def finish(sum_ref, amp_hbm, log_hbm, amp_v, log_v, sems):
    mine = amp_v.shape[1]
    peaks = sum_ref[:, mine:]
    first_peak = jnp.sqrt(peaks[0:1, 0:1]) + 1e-06
    second_peak = peaks[1:2, 0:1] / first_peak + 1e-06
    log_v[...] = jnp.log(first_peak) + jnp.log(second_peak)
    log_store = pltpu.make_async_copy(log_v, log_hbm, sems.at[0])
    log_store.start()
    amp_v[...] = sum_ref[:, :mine] * ((1.0 / LIFT) / first_peak) / second_peak
    amp_store = pltpu.make_async_copy(amp_v, amp_hbm, sems.at[1])
    amp_store.start()
    log_store.wait()
    amp_store.wait()


def shards(stem_tensor, branch_tensors, cut_values, bit_rows, bit_cols):
    n = lax.axis_size("cuts")
    slices = stem_tensor.shape[1]
    mine = bit_rows.shape[0] // n
    steps = branch_tensors.shape[0]
    any_spec = pl.BlockSpec(memory_space=pl.ANY)
    lined = (n, mine // LANES, LANES)
    sums = pl.pallas_call(
        functools.partial(kernel, n, 2),
        out_shape=pltpu.VMEM((2, mine + LANES), jnp.float32),
        in_specs=[any_spec] * 5,
        out_specs=pl.BlockSpec(memory_space=pltpu.VMEM),
        scratch_shapes=[
            pltpu.SMEM((steps, slices), jnp.int32),
            pltpu.VMEM(stem_tensor.shape, jnp.bfloat16),
            pltpu.VMEM(branch_tensors.shape[1:], jnp.bfloat16),
            pltpu.VMEM(branch_tensors.shape[1:], jnp.bfloat16),
            pltpu.VMEM(lined, jnp.int32),
            pltpu.VMEM(lined, jnp.int32),
            pltpu.VMEM((n, 2, mine + LANES), jnp.float32),
            pltpu.VMEM((n, 2, mine + LANES), jnp.float32),
            pltpu.SemaphoreType.DMA((4 + 4 * steps,)),
            pltpu.SemaphoreType.DMA,
            pltpu.SemaphoreType.DMA,
        ],
        compiler_params=pltpu.CompilerParams(
            collective_id=0, has_side_effects=True, vmem_limit_bytes=56 * 1024 * 1024
        ),
    )(cut_values.T, stem_tensor, branch_tensors, bit_rows.reshape(lined), bit_cols.reshape(lined))
    amplitudes, log_scale = pl.pallas_call(
        finish,
        out_shape=(
            jax.ShapeDtypeStruct((2, mine), jnp.float32),
            jax.ShapeDtypeStruct((1, 1), jnp.float32),
        ),
        in_specs=[pl.BlockSpec(memory_space=pltpu.VMEM)],
        out_specs=(any_spec, any_spec),
        scratch_shapes=[
            pltpu.VMEM((2, mine), jnp.float32),
            pltpu.VMEM((1, 1), jnp.float32),
            pltpu.SemaphoreType.DMA((2,)),
        ],
    )(pltpu.with_memory_space_constraint(sums, pltpu.VMEM))
    return (amplitudes, log_scale.reshape(1))


def solution(mesh):
    placed = (
        P(None, ("grp", "cuts"), None, None),
        P(),
        P(("grp", "cuts"), None),
        P("grp"),
        P("grp"),
    )
    return jax.shard_map(
        shards,
        mesh=mesh,
        in_specs=placed,
        out_specs=(P(None, ("grp", "cuts")), P("grp")),
        check_vma=False,
    )
```

```python
import functools

import jax
import jax.numpy as jnp
from jax import lax
from jax.experimental import pallas as pl
from jax.experimental.pallas import tpu as pltpu
from jax.sharding import PartitionSpec as P

LANES = 128
LIFT = 2.0 ** 20


def complex_step(parts, flags, matrices, loads):
    found = None
    for v in range(matrices.shape[0]):
        rows = []
        for (real_part, imag_part), flag in zip(parts, flags):
            real_now = real_part * flag[v]
            imag_now = imag_part * flag[v]
            for pair in ((real_now, -imag_now), (imag_now, real_now)):
                rows.append(jnp.concatenate(pair, axis=1))
        left = jnp.concatenate(rows, axis=0)
        for load in loads[v]:
            load.wait()
        _, kinds, depth, width = matrices.shape
        product = jnp.dot(left, matrices[v].reshape(kinds * depth, width), preferred_element_type=jnp.float32)
        found = product if found is None else found + product
    height = found.shape[0] // len(parts)
    return [found[s * height:(s + 1) * height] for s in range(len(parts))]


def largest(values):
    return jnp.max(jnp.max(values, axis=0, keepdims=True), axis=1, keepdims=True)


def kernel(n, group, cut_hbm, stem_hbm, branch_hbm, rows_hbm, cols_hbm, out_ref,
           cut_s, stem_v, early_v, later_v, rows_v, cols_v, outgoing, incoming, load_sems, send_sem, recv_sem):
    me = lax.axis_index("cuts")
    slices, rows, width = stem_hbm.shape[1], stem_hbm.shape[2], stem_hbm.shape[3]
    mine = out_ref.shape[1] - LANES
    lines = mine // LANES

    cols_load = pltpu.make_async_copy(cols_hbm, cols_v, load_sems.at[0])
    rows_load = pltpu.make_async_copy(rows_hbm, rows_v, load_sems.at[1])
    cut_load = pltpu.make_async_copy(cut_hbm, cut_s, load_sems.at[2])
    stem_load = pltpu.make_async_copy(stem_hbm, stem_v, load_sems.at[3])
    branch_loads = [
        [
            [
                pltpu.make_async_copy(
                    branch_hbm.at[step, value, part], held.at[value, part], load_sems.at[4 + 4 * step + 2 * value + part])
                for part in range(2)
            ]
            for value in range(2)
        ]
        for step, held in enumerate((early_v, later_v))
    ]
    for load in [cut_load, stem_load, *branch_loads[0][0], *branch_loads[0][1], cols_load, rows_load,
                 *branch_loads[1][0], *branch_loads[1][1]]:
        load.start()

    barrier = pltpu.get_barrier_semaphore()

    def greet(k, carry):
        pl.semaphore_signal(barrier, inc=1, device_id={"cuts": lax.rem(me + k, n)}, device_id_type=pl.DeviceIdType.MESH)
        return carry

    lax.fori_loop(1, n, greet, 0)

    def hot_columns(dest):
        col_lines = cols_v[dest]
        column = lax.broadcasted_iota(jnp.int16, (LANES, LANES), 0)
        one, zero = jnp.bfloat16(1), jnp.bfloat16(0)
        low_part = lax.rem(col_lines, LANES)
        lanes = [jnp.broadcast_to(low_part[j:j + 1], (LANES, LANES)).astype(jnp.int16) for j in range(lines)]
        return jnp.concatenate([jnp.where(column == line, one, zero) for line in lanes], axis=1)

    def nth_dest(i):
        return jnp.where(i >= n - 1, me, jnp.where(i >= me, i + 1, i))

    cut_load.wait()
    stem_load.wait()
    def flags(step):
        return [
            [jnp.full((1, 1), jnp.where(cut_s[step, s] == v, 1.0, 0.0)).astype(jnp.bfloat16) for v in range(2)]
            for s in range(slices)
        ]

    first = complex_step([(stem_v[0, s], stem_v[1, s]) for s in range(slices)], flags(0), early_v, branch_loads[0])
    cols_load.wait()
    rows_load.wait()
    states = [(p * LIFT).astype(jnp.bfloat16) for p in first]
    second = complex_step([(p[:rows], p[rows:]) for p in states], flags(1), later_v, branch_loads[1])

    square = functools.reduce(jnp.maximum, [p[:rows] * p[:rows] + p[rows:] * p[rows:] for p in first])
    peak_square = largest(square)
    own_peak = jnp.sqrt(peak_square) + 1e-06
    shrink = (1.0 / LIFT) / own_peak
    shrunk = [p * shrink for p in second]
    square = functools.reduce(jnp.maximum, [p[:rows] * p[:rows] + p[rows:] * p[rows:] for p in shrunk])
    raw_second = jnp.sqrt(largest(square)) * own_peak
    stats = jnp.concatenate(
        [jnp.broadcast_to(peak_square, (1, LANES)), jnp.broadcast_to(raw_second, (1, LANES))], axis=0)

    table = functools.reduce(jnp.add, second)
    high = table.astype(jnp.bfloat16)
    low = (table - high.astype(jnp.float32)).astype(jnp.bfloat16)
    blocks = width // LANES

    def blocked(half):
        return jnp.concatenate(
            [half[p * rows:(p + 1) * rows, c * LANES:(c + 1) * LANES] for p in range(2) for c in range(blocks)], axis=0)

    left = jnp.concatenate([blocked(high), blocked(low)], axis=1)

    def picked(dest):
        hot = hot_columns(dest)
        spots = blocks * rows
        spot_lines = (cols_v[dest] // LANES) * rows + rows_v[dest]
        spot = lax.broadcasted_iota(jnp.int32, (spots, LANES), 0)
        found = jnp.dot(left, jnp.concatenate([hot, hot], axis=0), preferred_element_type=jnp.float32)
        chosen = jnp.concatenate([spot == spot_lines[j:j + 1] for j in range(lines)], axis=1)
        parts = [jnp.sum(jnp.where(chosen, found[p * spots:(p + 1) * spots], 0.0), axis=0, keepdims=True) for p in range(2)]
        return jnp.concatenate(parts, axis=0)

    def remote(dest):
        return pltpu.make_async_remote_copy(
            src_ref=outgoing.at[dest],
            dst_ref=incoming.at[me],
            send_sem=send_sem,
            recv_sem=recv_sem,
            device_id={"cuts": dest},
            device_id_type=pl.DeviceIdType.MESH,
        )

    def serve(start, count):
        dests = [nth_dest(start + i) for i in range(count)]
        for dest in dests:
            outgoing[dest, :, :mine] = picked(dest)
            outgoing[dest, :, mine:] = stats
        if isinstance(start, int) and start == 0:
            pl.semaphore_wait(barrier, n - 1)
        for dest in dests:
            remote(dest).start()

    def serve_group(g, carry):
        serve(2 + g * group, group)
        return carry

    serve(0, 1)
    serve(1, 1)
    rounds = (n - 3) // group
    if n <= 16:
        for g in range(rounds):
            serve(2 + g * group, group)
    else:
        lax.fori_loop(0, rounds, serve_group, 0)
    serve(2 + rounds * group, n - 3 - rounds * group)
    incoming[me, :, :mine] = picked(me)
    incoming[me, :, mine:] = stats

    everything = pl.ds(0, n - 1)
    pltpu.make_async_copy(outgoing.at[everything], incoming.at[everything], recv_sem).wait()
    pltpu.make_async_copy(outgoing.at[everything], incoming.at[everything], send_sem).wait()
    out_ref[:, :mine] = jnp.sum(incoming[:, :, :mine], axis=0)
    out_ref[:, mine:] = jnp.max(incoming[:, :, mine:], axis=0)


def finish(sum_ref, amp_hbm, log_hbm, amp_v, log_v, sems):
    mine = amp_v.shape[1]
    peaks = sum_ref[:, mine:]
    first_peak = jnp.sqrt(peaks[0:1, 0:1]) + 1e-06
    second_peak = peaks[1:2, 0:1] / first_peak + 1e-06
    log_v[...] = jnp.log(first_peak) + jnp.log(second_peak)
    log_store = pltpu.make_async_copy(log_v, log_hbm, sems.at[0])
    log_store.start()
    amp_v[...] = sum_ref[:, :mine] * ((1.0 / LIFT) / first_peak) / second_peak
    amp_store = pltpu.make_async_copy(amp_v, amp_hbm, sems.at[1])
    amp_store.start()
    log_store.wait()
    amp_store.wait()


def shards(stem_tensor, branch_tensors, cut_values, bit_rows, bit_cols):
    n = lax.axis_size("cuts")
    slices = stem_tensor.shape[1]
    mine = bit_rows.shape[0] // n
    steps = branch_tensors.shape[0]
    any_spec = pl.BlockSpec(memory_space=pl.ANY)
    lined = (n, mine // LANES, LANES)
    sums = pl.pallas_call(
        functools.partial(kernel, n, 2),
        out_shape=pltpu.VMEM((2, mine + LANES), jnp.float32),
        in_specs=[any_spec] * 5,
        out_specs=pl.BlockSpec(memory_space=pltpu.VMEM),
        scratch_shapes=[
            pltpu.SMEM((steps, slices), jnp.int32),
            pltpu.VMEM(stem_tensor.shape, jnp.bfloat16),
            pltpu.VMEM(branch_tensors.shape[1:], jnp.bfloat16),
            pltpu.VMEM(branch_tensors.shape[1:], jnp.bfloat16),
            pltpu.VMEM(lined, jnp.int32),
            pltpu.VMEM(lined, jnp.int32),
            pltpu.VMEM((n, 2, mine + LANES), jnp.float32),
            pltpu.VMEM((n, 2, mine + LANES), jnp.float32),
            pltpu.SemaphoreType.DMA((4 + 4 * steps,)),
            pltpu.SemaphoreType.DMA,
            pltpu.SemaphoreType.DMA,
        ],
        compiler_params=pltpu.CompilerParams(
            collective_id=0, has_side_effects=True, vmem_limit_bytes=56 * 1024 * 1024
        ),
    )(cut_values.T, stem_tensor, branch_tensors, bit_rows.reshape(lined), bit_cols.reshape(lined))
    amplitudes, log_scale = pl.pallas_call(
        finish,
        out_shape=(
            jax.ShapeDtypeStruct((2, mine), jnp.float32),
            jax.ShapeDtypeStruct((1, 1), jnp.float32),
        ),
        in_specs=[pl.BlockSpec(memory_space=pltpu.VMEM)],
        out_specs=(any_spec, any_spec),
        scratch_shapes=[
            pltpu.VMEM((2, mine), jnp.float32),
            pltpu.VMEM((1, 1), jnp.float32),
            pltpu.SemaphoreType.DMA((2,)),
        ],
    )(pltpu.with_memory_space_constraint(sums, pltpu.VMEM))
    return (amplitudes, log_scale.reshape(1))


def solution(mesh):
    placed = (
        P(None, ("grp", "cuts"), None, None),
        P(),
        P(("grp", "cuts"), None),
        P("grp"),
        P("grp"),
    )
    return jax.shard_map(
        shards,
        mesh=mesh,
        in_specs=placed,
        out_specs=(P(None, ("grp", "cuts")), P("grp")),
        check_vma=False,
    )
```

```python
import functools

import jax
import jax.numpy as jnp
from jax import lax
from jax.experimental import pallas as pl
from jax.experimental.pallas import tpu as pltpu
from jax.sharding import PartitionSpec as P

LANES = 128
LIFT = 2.0 ** 20


def complex_step(parts, flags, matrices, loads):
    found = None
    for v in range(matrices.shape[0]):
        rows = []
        for (real_part, imag_part), flag in zip(parts, flags):
            real_now = real_part * flag[v]
            imag_now = imag_part * flag[v]
            for pair in ((real_now, -imag_now), (imag_now, real_now)):
                rows.append(jnp.concatenate([x.astype(jnp.bfloat16) for x in pair], axis=1))
        left = jnp.concatenate(rows, axis=0)
        for load in loads[v]:
            load.wait()
        _, kinds, depth, width = matrices.shape
        product = jnp.dot(left, matrices[v].reshape(kinds * depth, width), preferred_element_type=jnp.float32)
        found = product if found is None else found + product
    height = found.shape[0] // len(parts)
    return [found[s * height:(s + 1) * height] for s in range(len(parts))]


def largest(values):
    return jnp.max(jnp.max(values, axis=0, keepdims=True), axis=1, keepdims=True)


def kernel(n, group, cut_hbm, stem_hbm, branch_hbm, rows_hbm, cols_hbm, out_ref,
           cut_s, stem_v, early_v, later_v, rows_v, cols_v, outgoing, incoming, load_sems, send_sem, recv_sem):
    me = lax.axis_index("cuts")
    slices, rows, width = stem_hbm.shape[1], stem_hbm.shape[2], stem_hbm.shape[3]
    mine = out_ref.shape[1] - LANES
    lines = mine // LANES

    cols_load = pltpu.make_async_copy(cols_hbm, cols_v, load_sems.at[0])
    rows_load = pltpu.make_async_copy(rows_hbm, rows_v, load_sems.at[1])
    cut_load = pltpu.make_async_copy(cut_hbm, cut_s, load_sems.at[2])
    stem_load = pltpu.make_async_copy(stem_hbm, stem_v, load_sems.at[3])
    branch_loads = [
        [
            [
                pltpu.make_async_copy(
                    branch_hbm.at[step, value, part], held.at[value, part], load_sems.at[4 + 4 * step + 2 * value + part])
                for part in range(2)
            ]
            for value in range(2)
        ]
        for step, held in enumerate((early_v, later_v))
    ]
    for load in [cut_load, stem_load, *branch_loads[0][0], *branch_loads[0][1], cols_load, rows_load,
                 *branch_loads[1][0], *branch_loads[1][1]]:
        load.start()

    barrier = pltpu.get_barrier_semaphore()

    def greet(k, carry):
        pl.semaphore_signal(barrier, inc=1, device_id={"cuts": lax.rem(me + k, n)}, device_id_type=pl.DeviceIdType.MESH)
        return carry

    lax.fori_loop(1, n, greet, 0)

    def hot_columns(dest):
        col_lines = cols_v[dest]
        column = lax.broadcasted_iota(jnp.int16, (LANES, LANES), 0)
        one, zero = jnp.bfloat16(1), jnp.bfloat16(0)
        low_part = lax.rem(col_lines, LANES)
        lanes = [jnp.broadcast_to(low_part[j:j + 1], (LANES, LANES)).astype(jnp.int16) for j in range(lines)]
        return jnp.concatenate([jnp.where(column == line, one, zero) for line in lanes], axis=1)

    def nth_dest(i):
        return jnp.where(i >= n - 1, me, jnp.where(i >= me, i + 1, i))

    cut_load.wait()
    stem_load.wait()
    def flags(step, scale, dtype):
        return [
            [jnp.full((1, 1), jnp.where(cut_s[step, s] == v, scale, 0.0)).astype(dtype) for v in range(2)]
            for s in range(slices)
        ]

    first = complex_step(
        [(stem_v[0, s], stem_v[1, s]) for s in range(slices)], flags(0, 1.0, jnp.bfloat16), early_v, branch_loads[0])
    cols_load.wait()
    rows_load.wait()
    for load in branch_loads[1][0] + branch_loads[1][1]:
        load.wait()
    second = complex_step([(p[:rows], p[rows:]) for p in first], flags(1, LIFT, jnp.float32), later_v, [[], []])

    square = functools.reduce(jnp.maximum, [p[:rows] * p[:rows] + p[rows:] * p[rows:] for p in first])
    peak_square = largest(square)
    own_peak = jnp.sqrt(peak_square) + 1e-06
    shrink = (1.0 / LIFT) / own_peak
    shrunk = [p * shrink for p in second]
    square = functools.reduce(jnp.maximum, [p[:rows] * p[:rows] + p[rows:] * p[rows:] for p in shrunk])
    raw_second = jnp.sqrt(largest(square)) * own_peak
    stats = jnp.concatenate(
        [jnp.broadcast_to(peak_square, (1, LANES)), jnp.broadcast_to(raw_second, (1, LANES))], axis=0)

    table = functools.reduce(jnp.add, second)
    high = table.astype(jnp.bfloat16)
    low = (table - high.astype(jnp.float32)).astype(jnp.bfloat16)
    blocks = width // LANES

    def blocked(half):
        return jnp.concatenate(
            [half[p * rows:(p + 1) * rows, c * LANES:(c + 1) * LANES] for p in range(2) for c in range(blocks)], axis=0)

    left = jnp.concatenate([blocked(high), blocked(low)], axis=1)

    def picked(dest):
        hot = hot_columns(dest)
        spots = blocks * rows
        spot_lines = (cols_v[dest] // LANES) * rows + rows_v[dest]
        spot = lax.broadcasted_iota(jnp.int32, (spots, LANES), 0)
        found = jnp.dot(left, jnp.concatenate([hot, hot], axis=0), preferred_element_type=jnp.float32)
        chosen = jnp.concatenate([spot == spot_lines[j:j + 1] for j in range(lines)], axis=1)
        parts = [jnp.sum(jnp.where(chosen, found[p * spots:(p + 1) * spots], 0.0), axis=0, keepdims=True) for p in range(2)]
        return jnp.concatenate(parts, axis=0)

    def remote(dest):
        return pltpu.make_async_remote_copy(
            src_ref=outgoing.at[dest],
            dst_ref=incoming.at[me],
            send_sem=send_sem,
            recv_sem=recv_sem,
            device_id={"cuts": dest},
            device_id_type=pl.DeviceIdType.MESH,
        )

    def fill(dest):
        outgoing[dest, :, :mine] = picked(dest)
        outgoing[dest, :, mine:] = stats

    def serve(start, count):
        dests = [nth_dest(start + i) for i in range(count)]
        for dest in dests:
            fill(dest)
        if isinstance(start, int) and start == 0:
            pl.semaphore_wait(barrier, n - 1)
        for dest in dests:
            remote(dest).start()

    def keep_own():
        incoming[me, :, :mine] = picked(me)
        incoming[me, :, mine:] = stats

    @pl.when(me < n // 2)
    def _():
        lax.fori_loop(0, n - 1, lambda i, carry: (fill(nth_dest(i)), carry)[1], 0)
        keep_own()
        pl.semaphore_wait(barrier, n - 1)
        lax.fori_loop(0, n - 1, lambda i, carry: (remote(nth_dest(i)).start(), carry)[1], 0)

    @pl.when(me >= n // 2)
    def _():
        serve(0, group)
        rounds = (n - 1) // group
        if n <= 16:
            for g in range(1, rounds):
                serve(g * group, group)
        else:
            lax.fori_loop(1, rounds, lambda g, carry: (serve(g * group, group), carry)[1], 0)
        serve(rounds * group, n - 1 - rounds * group)
        keep_own()

    everything = pl.ds(0, n - 1)
    pltpu.make_async_copy(outgoing.at[everything], incoming.at[everything], recv_sem).wait()
    pltpu.make_async_copy(outgoing.at[everything], incoming.at[everything], send_sem).wait()
    out_ref[:, :mine] = jnp.sum(incoming[:, :, :mine], axis=0)
    out_ref[:, mine:] = jnp.max(incoming[:, :, mine:], axis=0)


def finish(sum_ref, amp_hbm, log_hbm, amp_v, log_v, sems):
    mine = amp_v.shape[1]
    peaks = sum_ref[:, mine:]
    first_peak = jnp.sqrt(peaks[0:1, 0:1]) + 1e-06
    second_peak = peaks[1:2, 0:1] / first_peak + 1e-06
    log_v[...] = jnp.log(first_peak) + jnp.log(second_peak)
    log_store = pltpu.make_async_copy(log_v, log_hbm, sems.at[0])
    log_store.start()
    amp_v[...] = sum_ref[:, :mine] * ((1.0 / LIFT) / first_peak) / second_peak
    amp_store = pltpu.make_async_copy(amp_v, amp_hbm, sems.at[1])
    amp_store.start()
    log_store.wait()
    amp_store.wait()


def shards(stem_tensor, branch_tensors, cut_values, bit_rows, bit_cols):
    n = lax.axis_size("cuts")
    slices = stem_tensor.shape[1]
    mine = bit_rows.shape[0] // n
    steps = branch_tensors.shape[0]
    any_spec = pl.BlockSpec(memory_space=pl.ANY)
    lined = (n, mine // LANES, LANES)
    sums = pl.pallas_call(
        functools.partial(kernel, n, 2),
        out_shape=pltpu.VMEM((2, mine + LANES), jnp.float32),
        in_specs=[any_spec] * 5,
        out_specs=pl.BlockSpec(memory_space=pltpu.VMEM),
        scratch_shapes=[
            pltpu.SMEM((steps, slices), jnp.int32),
            pltpu.VMEM(stem_tensor.shape, jnp.bfloat16),
            pltpu.VMEM(branch_tensors.shape[1:], jnp.bfloat16),
            pltpu.VMEM(branch_tensors.shape[1:], jnp.bfloat16),
            pltpu.VMEM(lined, jnp.int32),
            pltpu.VMEM(lined, jnp.int32),
            pltpu.VMEM((n, 2, mine + LANES), jnp.float32),
            pltpu.VMEM((n, 2, mine + LANES), jnp.float32),
            pltpu.SemaphoreType.DMA((4 + 4 * steps,)),
            pltpu.SemaphoreType.DMA,
            pltpu.SemaphoreType.DMA,
        ],
        compiler_params=pltpu.CompilerParams(
            collective_id=0, has_side_effects=True, vmem_limit_bytes=56 * 1024 * 1024
        ),
    )(cut_values.T, stem_tensor, branch_tensors, bit_rows.reshape(lined), bit_cols.reshape(lined))
    amplitudes, log_scale = pl.pallas_call(
        finish,
        out_shape=(
            jax.ShapeDtypeStruct((2, mine), jnp.float32),
            jax.ShapeDtypeStruct((1, 1), jnp.float32),
        ),
        in_specs=[pl.BlockSpec(memory_space=pltpu.VMEM)],
        out_specs=(any_spec, any_spec),
        scratch_shapes=[
            pltpu.VMEM((2, mine), jnp.float32),
            pltpu.VMEM((1, 1), jnp.float32),
            pltpu.SemaphoreType.DMA((2,)),
        ],
    )(pltpu.with_memory_space_constraint(sums, pltpu.VMEM))
    return (amplitudes, log_scale.reshape(1))


def solution(mesh):
    placed = (
        P(None, ("grp", "cuts"), None, None),
        P(),
        P(("grp", "cuts"), None),
        P("grp"),
        P("grp"),
    )
    return jax.shard_map(
        shards,
        mesh=mesh,
        in_specs=placed,
        out_specs=(P(None, ("grp", "cuts")), P("grp")),
        check_vma=False,
    )
```

```python
import functools

import jax
import jax.numpy as jnp
from jax import lax
from jax.experimental import pallas as pl
from jax.experimental.pallas import tpu as pltpu
from jax.sharding import PartitionSpec as P

LANES = 128
DEPTH = 256
LIFT = 2.0 ** 20


def complex_step(parts, flags, matrices, loads):
    found = None
    for v in range(matrices.shape[0]):
        rows = []
        for (real_part, imag_part), flag in zip(parts, flags):
            real_now = real_part * flag[v]
            imag_now = imag_part * flag[v]
            for pair in ((real_now, -imag_now), (imag_now, real_now)):
                rows.append(jnp.concatenate([x.astype(jnp.bfloat16) for x in pair], axis=1))
        left = jnp.concatenate(rows, axis=0)
        for load in loads[v]:
            load.wait()
        _, kinds, depth, width = matrices.shape
        product = jnp.dot(left, matrices[v].reshape(kinds * depth, width), preferred_element_type=jnp.float32)
        found = product if found is None else found + product
    height = found.shape[0] // len(parts)
    return [found[s * height:(s + 1) * height] for s in range(len(parts))]


def largest(values):
    return jnp.max(jnp.max(values, axis=0, keepdims=True), axis=1, keepdims=True)


def kernel(n, group, cut_hbm, stem_hbm, branch_hbm, rows_hbm, cols_hbm, out_ref,
           cut_s, stem_v, early_v, later_v, rows_v, cols_v, outgoing, incoming, load_sems, send_sem, recv_sem):
    me = lax.axis_index("cuts")
    slices, rows, width = stem_hbm.shape[1], stem_hbm.shape[2], stem_hbm.shape[3]
    mine = out_ref.shape[1] - LANES
    lines = mine // LANES

    cols_load = pltpu.make_async_copy(cols_hbm, cols_v, load_sems.at[0])
    rows_load = pltpu.make_async_copy(rows_hbm, rows_v, load_sems.at[1])
    cut_load = pltpu.make_async_copy(cut_hbm, cut_s, load_sems.at[2])
    stem_load = pltpu.make_async_copy(stem_hbm, stem_v, load_sems.at[3])
    branch_loads = [
        [
            [
                pltpu.make_async_copy(
                    branch_hbm.at[step, value, part], held.at[value, part], load_sems.at[4 + 4 * step + 2 * value + part])
                for part in range(2)
            ]
            for value in range(2)
        ]
        for step, held in enumerate((early_v, later_v))
    ]
    for load in [cut_load, stem_load, *branch_loads[0][0], *branch_loads[0][1], cols_load, rows_load,
                 *branch_loads[1][0], *branch_loads[1][1]]:
        load.start()

    barrier = pltpu.get_barrier_semaphore()

    def greet(k, carry):
        pl.semaphore_signal(barrier, inc=1, device_id={"cuts": lax.rem(me + k, n)}, device_id_type=pl.DeviceIdType.MESH)
        return carry

    lax.fori_loop(1, n, greet, 0)

    def hot_columns(dest):
        col_lines = cols_v[dest]
        column = lax.broadcasted_iota(jnp.int16, (DEPTH, LANES), 0)
        one, zero = jnp.bfloat16(1), jnp.bfloat16(0)
        low_part = lax.rem(col_lines, DEPTH)
        lanes = [jnp.broadcast_to(low_part[j:j + 1], (DEPTH, LANES)).astype(jnp.int16) for j in range(lines)]
        return jnp.concatenate([jnp.where(column == line, one, zero) for line in lanes], axis=1)

    def nth_dest(i):
        return jnp.where(i >= n - 1, me, jnp.where(i >= me, i + 1, i))

    cut_load.wait()
    stem_load.wait()
    def flags(step, scale, dtype):
        return [
            [jnp.full((1, 1), jnp.where(cut_s[step, s] == v, scale, 0.0)).astype(dtype) for v in range(2)]
            for s in range(slices)
        ]

    first = complex_step(
        [(stem_v[0, s], stem_v[1, s]) for s in range(slices)], flags(0, 1.0, jnp.bfloat16), early_v, branch_loads[0])
    cols_load.wait()
    rows_load.wait()
    for load in branch_loads[1][0] + branch_loads[1][1]:
        load.wait()
    second = complex_step([(p[:rows], p[rows:]) for p in first], flags(1, LIFT, jnp.float32), later_v, [[], []])

    square = functools.reduce(jnp.maximum, [p[:rows] * p[:rows] + p[rows:] * p[rows:] for p in first])
    peak_square = largest(square)
    own_peak = jnp.sqrt(peak_square) + 1e-06
    shrink = (1.0 / LIFT) / own_peak
    shrunk = [p * shrink for p in second]
    square = functools.reduce(jnp.maximum, [p[:rows] * p[:rows] + p[rows:] * p[rows:] for p in shrunk])
    raw_second = jnp.sqrt(largest(square)) * own_peak
    stats = jnp.concatenate(
        [jnp.broadcast_to(peak_square, (1, LANES)), jnp.broadcast_to(raw_second, (1, LANES))], axis=0)

    table = functools.reduce(jnp.add, second)
    rounded = table.astype(jnp.bfloat16)
    blocks = width // DEPTH
    left = jnp.concatenate(
        [rounded[p * rows:(p + 1) * rows, c * DEPTH:(c + 1) * DEPTH] for p in range(2) for c in range(blocks)], axis=0)

    def picked(dest):
        hot = hot_columns(dest)
        spots = blocks * rows
        spot_lines = (cols_v[dest] // DEPTH) * rows + rows_v[dest]
        spot = lax.broadcasted_iota(jnp.int32, (spots, LANES), 0)
        found = jnp.dot(left, hot, preferred_element_type=jnp.float32)
        chosen = jnp.concatenate([spot == spot_lines[j:j + 1] for j in range(lines)], axis=1)
        parts = [jnp.sum(jnp.where(chosen, found[p * spots:(p + 1) * spots], 0.0), axis=0, keepdims=True) for p in range(2)]
        return jnp.concatenate(parts, axis=0)

    def remote(dest):
        return pltpu.make_async_remote_copy(
            src_ref=outgoing.at[dest],
            dst_ref=incoming.at[me],
            send_sem=send_sem,
            recv_sem=recv_sem,
            device_id={"cuts": dest},
            device_id_type=pl.DeviceIdType.MESH,
        )

    def serve(start, count):
        dests = [nth_dest(start + i) for i in range(count)]
        for dest in dests:
            outgoing[dest, :, :mine] = picked(dest)
            outgoing[dest, :, mine:] = stats
        if isinstance(start, int) and start == 0:
            pl.semaphore_wait(barrier, n - 1)
        for dest in dests:
            remote(dest).start()

    head = (n - 2) % group + 1
    rounds = (n - 1 - head) // group
    serve(0, head)
    if n <= 16:
        for g in range(rounds):
            serve(head + g * group, group)
    else:
        lax.fori_loop(0, rounds, lambda g, carry: (serve(head + g * group, group), carry)[1], 0)
    incoming[me, :, :mine] = picked(me)
    incoming[me, :, mine:] = stats

    everything = pl.ds(0, n - 1)
    pltpu.make_async_copy(outgoing.at[everything], incoming.at[everything], recv_sem).wait()
    pltpu.make_async_copy(outgoing.at[everything], incoming.at[everything], send_sem).wait()
    out_ref[:, :mine] = jnp.sum(incoming[:, :, :mine], axis=0)
    out_ref[:, mine:] = jnp.max(incoming[:, :, mine:], axis=0)


def finish(sum_ref, amp_hbm, log_hbm, amp_v, log_v, sems):
    mine = amp_v.shape[1]
    peaks = sum_ref[:, mine:]
    first_peak = jnp.sqrt(peaks[0:1, 0:1]) + 1e-06
    second_peak = peaks[1:2, 0:1] / first_peak + 1e-06
    log_v[...] = jnp.log(first_peak) + jnp.log(second_peak)
    log_store = pltpu.make_async_copy(log_v, log_hbm, sems.at[0])
    log_store.start()
    amp_v[...] = sum_ref[:, :mine] * ((1.0 / LIFT) / first_peak) / second_peak
    amp_store = pltpu.make_async_copy(amp_v, amp_hbm, sems.at[1])
    amp_store.start()
    log_store.wait()
    amp_store.wait()


def shards(stem_tensor, branch_tensors, cut_values, bit_rows, bit_cols):
    n = lax.axis_size("cuts")
    slices = stem_tensor.shape[1]
    mine = bit_rows.shape[0] // n
    steps = branch_tensors.shape[0]
    any_spec = pl.BlockSpec(memory_space=pl.ANY)
    lined = (n, mine // LANES, LANES)
    sums = pl.pallas_call(
        functools.partial(kernel, n, 4),
        out_shape=pltpu.VMEM((2, mine + LANES), jnp.float32),
        in_specs=[any_spec] * 5,
        out_specs=pl.BlockSpec(memory_space=pltpu.VMEM),
        scratch_shapes=[
            pltpu.SMEM((steps, slices), jnp.int32),
            pltpu.VMEM(stem_tensor.shape, jnp.bfloat16),
            pltpu.VMEM(branch_tensors.shape[1:], jnp.bfloat16),
            pltpu.VMEM(branch_tensors.shape[1:], jnp.bfloat16),
            pltpu.VMEM(lined, jnp.int32),
            pltpu.VMEM(lined, jnp.int32),
            pltpu.VMEM((n, 2, mine + LANES), jnp.float32),
            pltpu.VMEM((n, 2, mine + LANES), jnp.float32),
            pltpu.SemaphoreType.DMA((4 + 4 * steps,)),
            pltpu.SemaphoreType.DMA,
            pltpu.SemaphoreType.DMA,
        ],
        compiler_params=pltpu.CompilerParams(
            collective_id=0, has_side_effects=True, vmem_limit_bytes=56 * 1024 * 1024
        ),
    )(cut_values.T, stem_tensor, branch_tensors, bit_rows.reshape(lined), bit_cols.reshape(lined))
    amplitudes, log_scale = pl.pallas_call(
        finish,
        out_shape=(
            jax.ShapeDtypeStruct((2, mine), jnp.float32),
            jax.ShapeDtypeStruct((1, 1), jnp.float32),
        ),
        in_specs=[pl.BlockSpec(memory_space=pltpu.VMEM)],
        out_specs=(any_spec, any_spec),
        scratch_shapes=[
            pltpu.VMEM((2, mine), jnp.float32),
            pltpu.VMEM((1, 1), jnp.float32),
            pltpu.SemaphoreType.DMA((2,)),
        ],
    )(pltpu.with_memory_space_constraint(sums, pltpu.VMEM))
    return (amplitudes, log_scale.reshape(1))


def solution(mesh):
    placed = (
        P(None, ("grp", "cuts"), None, None),
        P(),
        P(("grp", "cuts"), None),
        P("grp"),
        P("grp"),
    )
    return jax.shard_map(
        shards,
        mesh=mesh,
        in_specs=placed,
        out_specs=(P(None, ("grp", "cuts")), P("grp")),
        check_vma=False,
    )
```

```python
import functools

import jax
import jax.numpy as jnp
from jax import lax
from jax.experimental import pallas as pl
from jax.experimental.pallas import tpu as pltpu
from jax.sharding import PartitionSpec as P

LANES = 128
DEPTH = 256
LIFT = 2.0 ** 20


def complex_step(parts, flags, matrices, loads):
    found = None
    for v in range(matrices.shape[0]):
        rows = []
        for (real_part, imag_part), flag in zip(parts, flags):
            real_now = real_part * flag[v]
            imag_now = imag_part * flag[v]
            for pair in ((real_now, -imag_now), (imag_now, real_now)):
                rows.append(jnp.concatenate([x.astype(jnp.bfloat16) for x in pair], axis=1))
        left = jnp.concatenate(rows, axis=0)
        for load in loads[v]:
            load.wait()
        _, kinds, depth, width = matrices.shape
        product = jnp.dot(left, matrices[v].reshape(kinds * depth, width), preferred_element_type=jnp.float32)
        found = product if found is None else found + product
    height = found.shape[0] // len(parts)
    return [found[s * height:(s + 1) * height] for s in range(len(parts))]


def largest(values):
    return jnp.max(jnp.max(values, axis=0, keepdims=True), axis=1, keepdims=True)


def kernel(n, group, cut_hbm, stem_hbm, branch_hbm, rows_hbm, cols_hbm, out_ref,
           cut_s, stem_v, early_v, later_v, rows_v, cols_v, outgoing, incoming, load_sems, send_sem, recv_sem):
    me = lax.axis_index("cuts")
    slices, rows, width = stem_hbm.shape[1], stem_hbm.shape[2], stem_hbm.shape[3]
    mine = out_ref.shape[1] - LANES
    lines = mine // LANES

    cols_load = pltpu.make_async_copy(cols_hbm, cols_v, load_sems.at[0])
    rows_load = pltpu.make_async_copy(rows_hbm, rows_v, load_sems.at[1])
    cut_load = pltpu.make_async_copy(cut_hbm, cut_s, load_sems.at[2])
    stem_load = pltpu.make_async_copy(stem_hbm, stem_v, load_sems.at[3])
    half = width // 2
    branch_loads = [
        [
            [
                pltpu.make_async_copy(
                    branch_hbm.at[step, value, part, pl.ds(start, half)],
                    held.at[value, part, pl.ds(start, half)],
                    load_sems.at[4 + 8 * step + 4 * value + 2 * part + start // half])
                for part in range(2) for start in (0, half)
            ]
            for value in range(2)
        ]
        for step, held in enumerate((early_v, later_v))
    ]
    for load in [cut_load, stem_load, *branch_loads[0][0], *branch_loads[0][1], cols_load, rows_load,
                 *branch_loads[1][0], *branch_loads[1][1]]:
        load.start()

    barrier = pltpu.get_barrier_semaphore()

    def greet(k, carry):
        pl.semaphore_signal(barrier, inc=1, device_id={"cuts": lax.rem(me + k, n)}, device_id_type=pl.DeviceIdType.MESH)
        return carry

    lax.fori_loop(1, n, greet, 0, unroll=n <= 16)

    def hot_columns(dest):
        col_lines = cols_v[dest]
        column = lax.broadcasted_iota(jnp.int16, (DEPTH, LANES), 0)
        one, zero = jnp.bfloat16(1), jnp.bfloat16(0)
        low_part = lax.rem(col_lines, DEPTH)
        lanes = [jnp.broadcast_to(low_part[j:j + 1], (DEPTH, LANES)).astype(jnp.int16) for j in range(lines)]
        return jnp.concatenate([jnp.where(column == line, one, zero) for line in lanes], axis=1)

    def nth_dest(i):
        return jnp.where(i >= n - 1, me, jnp.where(i >= me, i + 1, i))

    cut_load.wait()
    stem_load.wait()
    def flags(step, scale, dtype):
        return [
            [jnp.full((1, 1), jnp.where(cut_s[step, s] == v, scale, 0.0)).astype(dtype) for v in range(2)]
            for s in range(slices)
        ]

    first = complex_step(
        [(stem_v[0, s], stem_v[1, s]) for s in range(slices)], flags(0, 1.0, jnp.bfloat16), early_v, branch_loads[0])
    cols_load.wait()
    rows_load.wait()
    for load in branch_loads[1][0] + branch_loads[1][1]:
        load.wait()
    second = complex_step([(p[:rows], p[rows:]) for p in first], flags(1, LIFT, jnp.float32), later_v, [[], []])

    square = functools.reduce(jnp.maximum, [p[:rows] * p[:rows] + p[rows:] * p[rows:] for p in first])
    peak_square = largest(square)
    own_peak = jnp.sqrt(peak_square) + 1e-06
    shrink = (1.0 / LIFT) / own_peak
    shrunk = [p * shrink for p in second]
    square = functools.reduce(jnp.maximum, [p[:rows] * p[:rows] + p[rows:] * p[rows:] for p in shrunk])
    raw_second = jnp.sqrt(largest(square)) * own_peak
    stats = jnp.concatenate(
        [jnp.broadcast_to(peak_square, (1, LANES)), jnp.broadcast_to(raw_second, (1, LANES))], axis=0)

    table = functools.reduce(jnp.add, second)
    rounded = table.astype(jnp.bfloat16)
    blocks = width // DEPTH
    left = jnp.concatenate(
        [rounded[p * rows:(p + 1) * rows, c * DEPTH:(c + 1) * DEPTH] for p in range(2) for c in range(blocks)], axis=0)

    def picked(dest):
        hot = hot_columns(dest)
        spots = blocks * rows
        spot_lines = (cols_v[dest] // DEPTH) * rows + rows_v[dest]
        spot = lax.broadcasted_iota(jnp.int32, (spots, LANES), 0)
        found = jnp.dot(left, hot, preferred_element_type=jnp.float32)
        chosen = jnp.concatenate([spot == spot_lines[j:j + 1] for j in range(lines)], axis=1)
        parts = [jnp.sum(jnp.where(chosen, found[p * spots:(p + 1) * spots], 0.0), axis=0, keepdims=True) for p in range(2)]
        return jnp.concatenate(parts, axis=0)

    def remote(dest):
        return pltpu.make_async_remote_copy(
            src_ref=outgoing.at[dest],
            dst_ref=incoming.at[me],
            send_sem=send_sem,
            recv_sem=recv_sem,
            device_id={"cuts": dest},
            device_id_type=pl.DeviceIdType.MESH,
        )

    def serve(start, count):
        dests = [nth_dest(start + i) for i in range(count)]
        for dest in dests:
            outgoing[dest, :, :mine] = picked(dest)
            outgoing[dest, :, mine:] = stats
        if isinstance(start, int) and start == 0:
            pl.semaphore_wait(barrier, n - 1)
        for dest in dests:
            remote(dest).start()

    serve(0, 1)
    head = 1 + (n - 2) % group
    serve(1, head - 1)
    rounds = (n - 1 - head) // group
    if n <= 16:
        for g in range(rounds):
            serve(head + g * group, group)
    else:
        lax.fori_loop(0, rounds, lambda g, carry: (serve(head + g * group, group), carry)[1], 0)
    incoming[me, :, :mine] = picked(me)
    incoming[me, :, mine:] = stats

    everything = pl.ds(0, n - 1)
    pltpu.make_async_copy(outgoing.at[everything], incoming.at[everything], recv_sem).wait()
    pltpu.make_async_copy(outgoing.at[everything], incoming.at[everything], send_sem).wait()
    out_ref[:, :mine] = jnp.sum(incoming[:, :, :mine], axis=0)
    out_ref[:, mine:] = jnp.max(incoming[:, :, mine:], axis=0)


def finish(sum_ref, amp_hbm, log_hbm, amp_v, log_v, sems):
    mine = amp_v.shape[1]
    peaks = sum_ref[:, mine:]
    first_peak = jnp.sqrt(peaks[0:1, 0:1]) + 1e-06
    second_peak = peaks[1:2, 0:1] / first_peak + 1e-06
    log_v[...] = jnp.log(first_peak) + jnp.log(second_peak)
    log_store = pltpu.make_async_copy(log_v, log_hbm, sems.at[0])
    log_store.start()
    amp_v[...] = sum_ref[:, :mine] * ((1.0 / LIFT) / first_peak) / second_peak
    amp_store = pltpu.make_async_copy(amp_v, amp_hbm, sems.at[1])
    amp_store.start()
    log_store.wait()
    amp_store.wait()


def shards(stem_tensor, branch_tensors, cut_values, bit_rows, bit_cols):
    n = lax.axis_size("cuts")
    slices = stem_tensor.shape[1]
    mine = bit_rows.shape[0] // n
    steps = branch_tensors.shape[0]
    any_spec = pl.BlockSpec(memory_space=pl.ANY)
    lined = (n, mine // LANES, LANES)
    sums = pl.pallas_call(
        functools.partial(kernel, n, 4),
        out_shape=pltpu.VMEM((2, mine + LANES), jnp.float32),
        in_specs=[any_spec] * 5,
        out_specs=pl.BlockSpec(memory_space=pltpu.VMEM),
        scratch_shapes=[
            pltpu.SMEM((steps, slices), jnp.int32),
            pltpu.VMEM(stem_tensor.shape, jnp.bfloat16),
            pltpu.VMEM(branch_tensors.shape[1:], jnp.bfloat16),
            pltpu.VMEM(branch_tensors.shape[1:], jnp.bfloat16),
            pltpu.VMEM(lined, jnp.int32),
            pltpu.VMEM(lined, jnp.int32),
            pltpu.VMEM((n, 2, mine + LANES), jnp.float32),
            pltpu.VMEM((n, 2, mine + LANES), jnp.float32),
            pltpu.SemaphoreType.DMA((4 + 8 * steps,)),
            pltpu.SemaphoreType.DMA,
            pltpu.SemaphoreType.DMA,
        ],
        compiler_params=pltpu.CompilerParams(
            collective_id=0, has_side_effects=True, vmem_limit_bytes=56 * 1024 * 1024
        ),
    )(cut_values.T, stem_tensor, branch_tensors, bit_rows.reshape(lined), bit_cols.reshape(lined))
    amplitudes, log_scale = pl.pallas_call(
        finish,
        out_shape=(
            jax.ShapeDtypeStruct((2, mine), jnp.float32),
            jax.ShapeDtypeStruct((1, 1), jnp.float32),
        ),
        in_specs=[pl.BlockSpec(memory_space=pltpu.VMEM)],
        out_specs=(any_spec, any_spec),
        scratch_shapes=[
            pltpu.VMEM((2, mine), jnp.float32),
            pltpu.VMEM((1, 1), jnp.float32),
            pltpu.SemaphoreType.DMA((2,)),
        ],
    )(pltpu.with_memory_space_constraint(sums, pltpu.VMEM))
    return (amplitudes, log_scale.reshape(1))


def solution(mesh):
    placed = (
        P(None, ("grp", "cuts"), None, None),
        P(),
        P(("grp", "cuts"), None),
        P("grp"),
        P("grp"),
    )
    return jax.shard_map(
        shards,
        mesh=mesh,
        in_specs=placed,
        out_specs=(P(None, ("grp", "cuts")), P("grp")),
        check_vma=False,
    )
```

```python
import functools

import jax
import jax.numpy as jnp
from jax import lax
from jax.experimental import pallas as pl
from jax.experimental.pallas import tpu as pltpu
from jax.sharding import PartitionSpec as P

LANES = 128
DEPTH = 256
LIFT = 2.0 ** 20


def complex_step(parts, flags, matrices, loads):
    found = None
    for v in range(matrices.shape[0]):
        rows = []
        for (real_part, imag_part), flag in zip(parts, flags):
            real_now = real_part * flag[v]
            imag_now = imag_part * flag[v]
            for pair in ((real_now, -imag_now), (imag_now, real_now)):
                rows.append(jnp.concatenate([x.astype(jnp.bfloat16) for x in pair], axis=1))
        left = jnp.concatenate(rows, axis=0)
        for load in loads[v]:
            load.wait()
        _, kinds, depth, width = matrices.shape
        product = jnp.dot(left, matrices[v].reshape(kinds * depth, width), preferred_element_type=jnp.float32)
        found = product if found is None else found + product
    height = found.shape[0] // len(parts)
    return [found[s * height:(s + 1) * height] for s in range(len(parts))]


def largest(values):
    return jnp.max(jnp.max(values, axis=0, keepdims=True), axis=1, keepdims=True)


def kernel(n, group, cut_hbm, stem_hbm, branch_hbm, rows_hbm, cols_hbm, out_ref,
           cut_s, stem_v, early_v, later_v, rows_v, cols_v, outgoing, incoming, load_sems, send_sem, recv_sem):
    me = lax.axis_index("cuts")
    slices, rows, width = stem_hbm.shape[1], stem_hbm.shape[2], stem_hbm.shape[3]
    mine = out_ref.shape[1] - LANES
    lines = mine // LANES

    cols_load = pltpu.make_async_copy(cols_hbm, cols_v, load_sems.at[0])
    rows_load = pltpu.make_async_copy(rows_hbm, rows_v, load_sems.at[1])
    cut_load = pltpu.make_async_copy(cut_hbm, cut_s, load_sems.at[2])
    stem_load = pltpu.make_async_copy(stem_hbm, stem_v, load_sems.at[3])
    cut = width // 4
    branch_loads = [
        [
            [
                pltpu.make_async_copy(
                    branch_hbm.at[step, value, part, pl.ds(start, cut)],
                    held.at[value, part, pl.ds(start, cut)],
                    load_sems.at[4 + 16 * step + 8 * value + 4 * part + start // cut])
                for part in range(2) for start in range(0, width, cut)
            ]
            for value in range(2)
        ]
        for step, held in enumerate((early_v, later_v))
    ]
    for load in [cut_load, stem_load, *branch_loads[0][0], *branch_loads[0][1], cols_load, rows_load,
                 *branch_loads[1][0], *branch_loads[1][1]]:
        load.start()

    barrier = pltpu.get_barrier_semaphore()

    def greet(k, carry):
        pl.semaphore_signal(barrier, inc=1, device_id={"cuts": lax.rem(me + k, n)}, device_id_type=pl.DeviceIdType.MESH)
        return carry

    lax.fori_loop(1, n, greet, 0, unroll=n <= 16)

    def hot_columns(dest):
        col_lines = cols_v[dest]
        column = lax.broadcasted_iota(jnp.int16, (DEPTH, LANES), 0)
        one, zero = jnp.bfloat16(1), jnp.bfloat16(0)
        low_part = lax.rem(col_lines, DEPTH)
        lanes = [jnp.broadcast_to(low_part[j:j + 1], (DEPTH, LANES)).astype(jnp.int16) for j in range(lines)]
        return jnp.concatenate([jnp.where(column == line, one, zero) for line in lanes], axis=1)

    def nth_dest(i):
        return jnp.where(i >= n - 1, me, jnp.where(i >= me, i + 1, i))

    cut_load.wait()
    stem_load.wait()
    def flags(step, scale, dtype):
        return [
            [jnp.full((1, 1), jnp.where(cut_s[step, s] == v, scale, 0.0)).astype(dtype) for v in range(2)]
            for s in range(slices)
        ]

    first = complex_step(
        [(stem_v[0, s], stem_v[1, s]) for s in range(slices)], flags(0, 1.0, jnp.bfloat16), early_v, branch_loads[0])
    cols_load.wait()
    rows_load.wait()
    second = complex_step([(p[:rows], p[rows:]) for p in first], flags(1, LIFT, jnp.float32), later_v, branch_loads[1])

    square = functools.reduce(jnp.maximum, [p[:rows] * p[:rows] + p[rows:] * p[rows:] for p in first])
    peak_square = largest(square)
    own_peak = jnp.sqrt(peak_square) + 1e-06
    shrink = (1.0 / LIFT) / own_peak
    shrunk = [p * shrink for p in second]
    square = functools.reduce(jnp.maximum, [p[:rows] * p[:rows] + p[rows:] * p[rows:] for p in shrunk])
    raw_second = jnp.sqrt(largest(square)) * own_peak
    stats = jnp.concatenate(
        [jnp.broadcast_to(peak_square, (1, LANES)), jnp.broadcast_to(raw_second, (1, LANES))], axis=0)

    table = functools.reduce(jnp.add, second)
    rounded = table.astype(jnp.bfloat16)
    blocks = width // DEPTH
    left = jnp.concatenate(
        [rounded[p * rows:(p + 1) * rows, c * DEPTH:(c + 1) * DEPTH] for p in range(2) for c in range(blocks)], axis=0)

    def picked(dest):
        hot = hot_columns(dest)
        spots = blocks * rows
        spot_lines = (cols_v[dest] // DEPTH) * rows + rows_v[dest]
        spot = lax.broadcasted_iota(jnp.int32, (spots, LANES), 0)
        found = jnp.dot(left, hot, preferred_element_type=jnp.float32)
        chosen = jnp.concatenate([spot == spot_lines[j:j + 1] for j in range(lines)], axis=1)
        parts = [jnp.sum(jnp.where(chosen, found[p * spots:(p + 1) * spots], 0.0), axis=0, keepdims=True) for p in range(2)]
        return jnp.concatenate(parts, axis=0)

    def remote(dest):
        return pltpu.make_async_remote_copy(
            src_ref=outgoing.at[dest],
            dst_ref=incoming.at[me],
            send_sem=send_sem,
            recv_sem=recv_sem,
            device_id={"cuts": dest},
            device_id_type=pl.DeviceIdType.MESH,
        )

    def serve(start, count):
        dests = [nth_dest(start + i) for i in range(count)]
        for dest in dests:
            outgoing[dest, :, :mine] = picked(dest)
            outgoing[dest, :, mine:] = stats
        if isinstance(start, int) and start == 0:
            pl.semaphore_wait(barrier, n - 1)
        for dest in dests:
            remote(dest).start()

    serve(0, 1)
    head = 1 + (n - 2) % group
    serve(1, head - 1)
    rounds = (n - 1 - head) // group
    if n <= 16:
        for g in range(rounds):
            serve(head + g * group, group)
    else:
        lax.fori_loop(0, rounds, lambda g, carry: (serve(head + g * group, group), carry)[1], 0)
    incoming[me, :, :mine] = picked(me)
    incoming[me, :, mine:] = stats

    everything = pl.ds(0, n - 1)
    pltpu.make_async_copy(outgoing.at[everything], incoming.at[everything], recv_sem).wait()
    pltpu.make_async_copy(outgoing.at[everything], incoming.at[everything], send_sem).wait()
    out_ref[:, :mine] = jnp.sum(incoming[:, :, :mine], axis=0)
    out_ref[:, mine:] = jnp.max(incoming[:, :, mine:], axis=0)


def finish(sum_ref, amp_hbm, log_hbm, amp_v, log_v, sems):
    mine = amp_v.shape[1]
    peaks = sum_ref[:, mine:]
    first_peak = jnp.sqrt(peaks[0:1, 0:1]) + 1e-06
    second_peak = peaks[1:2, 0:1] / first_peak + 1e-06
    log_v[...] = jnp.log(first_peak) + jnp.log(second_peak)
    log_store = pltpu.make_async_copy(log_v, log_hbm, sems.at[0])
    log_store.start()
    amp_v[...] = sum_ref[:, :mine] * ((1.0 / LIFT) / first_peak) / second_peak
    amp_store = pltpu.make_async_copy(amp_v, amp_hbm, sems.at[1])
    amp_store.start()
    log_store.wait()
    amp_store.wait()


def shards(stem_tensor, branch_tensors, cut_values, bit_rows, bit_cols):
    n = lax.axis_size("cuts")
    slices = stem_tensor.shape[1]
    mine = bit_rows.shape[0] // n
    steps = branch_tensors.shape[0]
    any_spec = pl.BlockSpec(memory_space=pl.ANY)
    lined = (n, mine // LANES, LANES)
    sums = pl.pallas_call(
        functools.partial(kernel, n, 4),
        out_shape=pltpu.VMEM((2, mine + LANES), jnp.float32),
        in_specs=[any_spec] * 5,
        out_specs=pl.BlockSpec(memory_space=pltpu.VMEM),
        scratch_shapes=[
            pltpu.SMEM((steps, slices), jnp.int32),
            pltpu.VMEM(stem_tensor.shape, jnp.bfloat16),
            pltpu.VMEM(branch_tensors.shape[1:], jnp.bfloat16),
            pltpu.VMEM(branch_tensors.shape[1:], jnp.bfloat16),
            pltpu.VMEM(lined, jnp.int32),
            pltpu.VMEM(lined, jnp.int32),
            pltpu.VMEM((n, 2, mine + LANES), jnp.float32),
            pltpu.VMEM((n, 2, mine + LANES), jnp.float32),
            pltpu.SemaphoreType.DMA((4 + 16 * steps,)),
            pltpu.SemaphoreType.DMA,
            pltpu.SemaphoreType.DMA,
        ],
        compiler_params=pltpu.CompilerParams(
            collective_id=0, has_side_effects=True, vmem_limit_bytes=56 * 1024 * 1024
        ),
    )(cut_values.T, stem_tensor, branch_tensors, bit_rows.reshape(lined), bit_cols.reshape(lined))
    amplitudes, log_scale = pl.pallas_call(
        finish,
        out_shape=(
            jax.ShapeDtypeStruct((2, mine), jnp.float32),
            jax.ShapeDtypeStruct((1, 1), jnp.float32),
        ),
        in_specs=[pl.BlockSpec(memory_space=pltpu.VMEM)],
        out_specs=(any_spec, any_spec),
        scratch_shapes=[
            pltpu.VMEM((2, mine), jnp.float32),
            pltpu.VMEM((1, 1), jnp.float32),
            pltpu.SemaphoreType.DMA((2,)),
        ],
    )(pltpu.with_memory_space_constraint(sums, pltpu.VMEM))
    return (amplitudes, log_scale.reshape(1))


def solution(mesh):
    placed = (
        P(None, ("grp", "cuts"), None, None),
        P(),
        P(("grp", "cuts"), None),
        P("grp"),
        P("grp"),
    )
    return jax.shard_map(
        shards,
        mesh=mesh,
        in_specs=placed,
        out_specs=(P(None, ("grp", "cuts")), P("grp")),
        check_vma=False,
    )
```

```python
import functools

import jax
import jax.numpy as jnp
from jax import lax
from jax.experimental import pallas as pl
from jax.experimental.pallas import tpu as pltpu
from jax.sharding import PartitionSpec as P

LANES = 128
DEPTH = 256
LIFT = 2.0 ** 20


def complex_step(parts, flags, matrices, loads):
    found = None
    for v in range(matrices.shape[0]):
        rows = []
        for (real_part, imag_part), flag in zip(parts, flags):
            real_now = real_part * flag[v]
            imag_now = imag_part * flag[v]
            for pair in ((real_now, -imag_now), (imag_now, real_now)):
                rows.append(jnp.concatenate([x.astype(jnp.bfloat16) for x in pair], axis=1))
        left = jnp.concatenate(rows, axis=0)
        for load in loads[v]:
            load.wait()
        _, kinds, depth, width = matrices.shape
        product = jnp.dot(left, matrices[v].reshape(kinds * depth, width), preferred_element_type=jnp.float32)
        found = product if found is None else found + product
    height = found.shape[0] // len(parts)
    return [found[s * height:(s + 1) * height] for s in range(len(parts))]


def largest(values):
    return jnp.max(jnp.max(values, axis=0, keepdims=True), axis=1, keepdims=True)


def kernel(n, group, cut_hbm, stem_hbm, branch_hbm, rows_hbm, cols_hbm, out_ref,
           cut_s, stem_v, early_v, later_v, rows_v, cols_v, outgoing, incoming, load_sems, send_sem, recv_sem):
    me = lax.axis_index("cuts")
    slices, rows, width = stem_hbm.shape[1], stem_hbm.shape[2], stem_hbm.shape[3]
    mine = out_ref.shape[1] - LANES
    lines = mine // LANES

    cols_load = pltpu.make_async_copy(cols_hbm, cols_v, load_sems.at[0])
    rows_load = pltpu.make_async_copy(rows_hbm, rows_v, load_sems.at[1])
    cut_load = pltpu.make_async_copy(cut_hbm, cut_s, load_sems.at[2])
    stem_load = pltpu.make_async_copy(stem_hbm, stem_v, load_sems.at[3])
    branch_loads = [
        [
            [pltpu.make_async_copy(branch_hbm.at[step, value], held.at[value], load_sems.at[4 + 2 * step + value])]
            for value in range(2)
        ]
        for step, held in enumerate((early_v, later_v))
    ]
    for load in [cut_load, stem_load, *branch_loads[0][0], *branch_loads[0][1], cols_load, rows_load,
                 *branch_loads[1][0], *branch_loads[1][1]]:
        load.start()

    barrier = pltpu.get_barrier_semaphore()

    def greet(k, carry):
        pl.semaphore_signal(barrier, inc=1, device_id={"cuts": lax.rem(me + k, n)}, device_id_type=pl.DeviceIdType.MESH)
        return carry

    lax.fori_loop(1, n, greet, 0, unroll=n <= 16)

    def hot_columns(dest):
        col_lines = cols_v[dest]
        column = lax.broadcasted_iota(jnp.int16, (DEPTH, LANES), 0)
        one, zero = jnp.bfloat16(1), jnp.bfloat16(0)
        low_part = lax.rem(col_lines, DEPTH)
        lanes = [jnp.broadcast_to(low_part[j:j + 1], (DEPTH, LANES)).astype(jnp.int16) for j in range(lines)]
        return jnp.concatenate([jnp.where(column == line, one, zero) for line in lanes], axis=1)

    def nth_dest(i):
        return jnp.where(i >= n - 1, me, jnp.where(i >= me, i + 1, i))

    cut_load.wait()
    stem_load.wait()
    def flags(step, scale, dtype):
        return [
            [jnp.full((1, 1), jnp.where(cut_s[step, s] == v, scale, 0.0)).astype(dtype) for v in range(2)]
            for s in range(slices)
        ]

    first = complex_step(
        [(stem_v[0, s], stem_v[1, s]) for s in range(slices)], flags(0, 1.0, jnp.bfloat16), early_v, branch_loads[0])
    cols_load.wait()
    rows_load.wait()
    for load in branch_loads[1][0] + branch_loads[1][1]:
        load.wait()
    second = complex_step([(p[:rows], p[rows:]) for p in first], flags(1, LIFT, jnp.float32), later_v, [[], []])

    square = functools.reduce(jnp.maximum, [p[:rows] * p[:rows] + p[rows:] * p[rows:] for p in first])
    peak_square = largest(square)
    own_peak = jnp.sqrt(peak_square) + 1e-06
    shrink = (1.0 / LIFT) / own_peak
    shrunk = [p * shrink for p in second]
    square = functools.reduce(jnp.maximum, [p[:rows] * p[:rows] + p[rows:] * p[rows:] for p in shrunk])
    raw_second = jnp.sqrt(largest(square)) * own_peak
    stats = jnp.concatenate(
        [jnp.broadcast_to(peak_square, (1, LANES)), jnp.broadcast_to(raw_second, (1, LANES))], axis=0)

    table = functools.reduce(jnp.add, second)
    rounded = table.astype(jnp.bfloat16)
    blocks = width // DEPTH
    left = jnp.concatenate(
        [rounded[p * rows:(p + 1) * rows, c * DEPTH:(c + 1) * DEPTH] for p in range(2) for c in range(blocks)], axis=0)

    def picked(dest):
        hot = hot_columns(dest)
        spots = blocks * rows
        spot_lines = (cols_v[dest] // DEPTH) * rows + rows_v[dest]
        spot = lax.broadcasted_iota(jnp.int32, (spots, LANES), 0)
        found = jnp.dot(left, hot, preferred_element_type=jnp.float32)
        chosen = jnp.concatenate([spot == spot_lines[j:j + 1] for j in range(lines)], axis=1)
        parts = [jnp.sum(jnp.where(chosen, found[p * spots:(p + 1) * spots], 0.0), axis=0, keepdims=True) for p in range(2)]
        return jnp.concatenate(parts, axis=0)

    def remote(dest):
        return pltpu.make_async_remote_copy(
            src_ref=outgoing.at[dest],
            dst_ref=incoming.at[me],
            send_sem=send_sem,
            recv_sem=recv_sem,
            device_id={"cuts": dest},
            device_id_type=pl.DeviceIdType.MESH,
        )

    def serve(start, count):
        dests = [nth_dest(start + i) for i in range(count)]
        for dest in dests:
            outgoing[dest, :, :mine] = picked(dest)
            outgoing[dest, :, mine:] = stats
        if isinstance(start, int) and start == 0:
            pl.semaphore_wait(barrier, n - 1)
        for dest in dests:
            remote(dest).start()

    serve(0, 1)
    head = 1 + (n - 2) % group
    serve(1, head - 1)
    rounds = (n - 1 - head) // group
    if n <= 16:
        for g in range(rounds):
            serve(head + g * group, group)
    else:
        lax.fori_loop(0, rounds, lambda g, carry: (serve(head + g * group, group), carry)[1], 0)
    incoming[me, :, :mine] = picked(me)
    incoming[me, :, mine:] = stats

    everything = pl.ds(0, n - 1)
    pltpu.make_async_copy(outgoing.at[everything], incoming.at[everything], recv_sem).wait()
    pltpu.make_async_copy(outgoing.at[everything], incoming.at[everything], send_sem).wait()
    out_ref[:, :mine] = jnp.sum(incoming[:, :, :mine], axis=0)
    out_ref[:, mine:] = jnp.max(incoming[:, :, mine:], axis=0)


def finish(sum_ref, amp_hbm, log_hbm, amp_v, log_v, sems):
    mine = amp_v.shape[1]
    peaks = sum_ref[:, mine:]
    first_peak = jnp.sqrt(peaks[0:1, 0:1]) + 1e-06
    second_peak = peaks[1:2, 0:1] / first_peak + 1e-06
    log_v[...] = jnp.log(first_peak) + jnp.log(second_peak)
    log_store = pltpu.make_async_copy(log_v, log_hbm, sems.at[0])
    log_store.start()
    amp_v[...] = sum_ref[:, :mine] * ((1.0 / LIFT) / first_peak) / second_peak
    amp_store = pltpu.make_async_copy(amp_v, amp_hbm, sems.at[1])
    amp_store.start()
    log_store.wait()
    amp_store.wait()


def shards(stem_tensor, branch_tensors, cut_values, bit_rows, bit_cols):
    n = lax.axis_size("cuts")
    slices = stem_tensor.shape[1]
    mine = bit_rows.shape[0] // n
    steps = branch_tensors.shape[0]
    any_spec = pl.BlockSpec(memory_space=pl.ANY)
    lined = (n, mine // LANES, LANES)
    sums = pl.pallas_call(
        functools.partial(kernel, n, 4),
        out_shape=pltpu.VMEM((2, mine + LANES), jnp.float32),
        in_specs=[any_spec] * 5,
        out_specs=pl.BlockSpec(memory_space=pltpu.VMEM),
        scratch_shapes=[
            pltpu.SMEM((steps, slices), jnp.int32),
            pltpu.VMEM(stem_tensor.shape, jnp.bfloat16),
            pltpu.VMEM(branch_tensors.shape[1:], jnp.bfloat16),
            pltpu.VMEM(branch_tensors.shape[1:], jnp.bfloat16),
            pltpu.VMEM(lined, jnp.int32),
            pltpu.VMEM(lined, jnp.int32),
            pltpu.VMEM((n, 2, mine + LANES), jnp.float32),
            pltpu.VMEM((n, 2, mine + LANES), jnp.float32),
            pltpu.SemaphoreType.DMA((4 + 2 * steps,)),
            pltpu.SemaphoreType.DMA,
            pltpu.SemaphoreType.DMA,
        ],
        compiler_params=pltpu.CompilerParams(
            collective_id=0, has_side_effects=True, vmem_limit_bytes=56 * 1024 * 1024
        ),
    )(cut_values.T, stem_tensor, branch_tensors, bit_rows.reshape(lined), bit_cols.reshape(lined))
    amplitudes, log_scale = pl.pallas_call(
        finish,
        out_shape=(
            jax.ShapeDtypeStruct((2, mine), jnp.float32),
            jax.ShapeDtypeStruct((1, 1), jnp.float32),
        ),
        in_specs=[pl.BlockSpec(memory_space=pltpu.VMEM)],
        out_specs=(any_spec, any_spec),
        scratch_shapes=[
            pltpu.VMEM((2, mine), jnp.float32),
            pltpu.VMEM((1, 1), jnp.float32),
            pltpu.SemaphoreType.DMA((2,)),
        ],
    )(pltpu.with_memory_space_constraint(sums, pltpu.VMEM))
    return (amplitudes, log_scale.reshape(1))


def solution(mesh):
    placed = (
        P(None, ("grp", "cuts"), None, None),
        P(),
        P(("grp", "cuts"), None),
        P("grp"),
        P("grp"),
    )
    return jax.shard_map(
        shards,
        mesh=mesh,
        in_specs=placed,
        out_specs=(P(None, ("grp", "cuts")), P("grp")),
        check_vma=False,
    )
```
